128 devices in a mesh: patch: 64 (over x_lo, y, z, core), head: 2 (over x_hi).
Axes of the slice: x: 4 (x_hi: 2, x_lo: 2; x = x_hi * 2 + x_lo), y: 4, z: 4, core: 2. Of those that a mesh axis runs over, the one named last changes fastest.
Arguments:
- image_hidden: bfloat16 [11264, 3072], P('patch', 'head'), may hold values from -6 to 6
- mod_table: float32 [28, 3, 3072], replicated, may hold values from -3 to 3
- step_index: int32 [1], replicated, may hold values from 0 to 27
- qkv_weight: bfloat16 [3072, 3, 1536], P(None, None, 'head'), may hold values from -0.109375 to 0.109375
- norm_gain: float32 [2, 128], replicated, may hold values from 0.1 to 24
- proj_weight: bfloat16 [1536, 3072], P('head'), may hold values from -0.15625 to 0.15625
- stale_kv: bfloat16 [2, 11264, 1536], P(None, 'patch', 'head'), may hold values from -64 to 64
- text_kv: bfloat16 [2, 512, 1536], P(None, 'patch', 'head'), may hold values from -16 to 16
- patch_order: int32 [64], replicated, may hold values from 0 to 63, each once
Outputs:
- image_out: bfloat16 [11264, 3072], P('patch', 'head')
- fresh_kv: bfloat16 [2, 11264, 1536], P(None, 'patch', 'head')
The draws below stay inside these ranges and needn't reach their ends.
Inputs may be any that keep to these rules, and one draw needn't show every extreme that they name: `patch_order`: each block index appears once.
All inputs are finite; a program needn't handle non-finite values.
Results may differ from the reference program's by a relative error of at most 0.013.
The reference program's roundings to bfloat16 on the way count: a program that leaves them out, or rounds other values in their place, can miss the bound.
Values may be sent and summed in bfloat16 or wider, within the bound.
A program may use at most 256 MiB of HBM per device.

```python
import jax
import jax.numpy as jnp
from jax import lax

D = 3072
HEADS = 12
HEAD_DIM = 128
TOK_DEV = 176
ROW_LEN = 256
STEPS = 28
IMG = 11264
TXT = 512
N_PATCH = 64


def draw_norm_gain(key, part):
    key = jax.random.fold_in(key, 11)
    noise = jnp.clip(jax.random.normal(key, (2, HEAD_DIM), jnp.float32), -5.0, 5.0)
    return 1.0 + 0.18 * noise


def draw_stale_kv(key, part):
    key = jax.random.fold_in(key, 23)
    width = HEADS * HEAD_DIM
    return (3.0 * jnp.clip(jax.random.normal(key, (2, IMG, width), jnp.float32), -5.3, 5.3)).astype(jnp.bfloat16)


def level_of(stream_key, shape, cuts, low, top_value):
    def one(dim, shards_of):
        heights = jax.random.uniform(jax.random.fold_in(jax.random.fold_in(stream_key, 6), dim), (shards_of,), jnp.float32, low / len(cuts), top_value / len(cuts))
        return jnp.repeat(jnp.exp(heights), shape[dim] // shards_of).reshape((-1,) + (1,) * (len(shape) - dim - 1))

    factor_of = one(*cuts[0])
    for cut in cuts[1:]:
        factor_of = factor_of * one(*cut)
    return factor_of


def normal_values(stream_key, dims, scale, most, shards=(), kind=jnp.bfloat16):
    drawn = jax.random.normal(stream_key, dims, jnp.float32) * scale
    if len(shards) > 0:
        drawn = level_of(stream_key, dims, shards, -0.22, 0.18) * drawn
    return jnp.clip(drawn, min=-most, max=most).astype(kind)


def setup_inputs(seed: int = 0) -> dict:
    seeds = jax.random.split(jax.random.key(seed), 10)
    return {
        "image_hidden": normal_values(seeds[0], (IMG, D), 1.0, 6.0, ((0, 64), (1, 2))),
        "mod_table": normal_values(seeds[1], (STEPS, 3, D), 0.5, 3.0, (), jnp.float32),
        "step_index": jax.random.randint(seeds[2], (1,), 0, STEPS).astype(jnp.int32),
        "qkv_weight": normal_values(seeds[3], (D, 3, HEADS * HEAD_DIM), D ** -0.5, 0.109375, ((2, 2),)),
        "norm_gain": draw_norm_gain(jax.random.fold_in(seeds[9], 71), 0),
        "proj_weight": normal_values(seeds[5], (HEADS * HEAD_DIM, D), (HEADS * HEAD_DIM) ** -0.5, 0.15625, ((0, 2),)),
        "stale_kv": draw_stale_kv(jax.random.fold_in(seeds[9], 71), 0),
        "text_kv": normal_values(seeds[7], (2, TXT, HEADS * HEAD_DIM), 3.0, 16.0, ((1, 64), (2, 2))),
        "patch_order": jax.random.permutation(seeds[8], N_PATCH).astype(jnp.int32),
    }


def rope_tables(positions):
    row_pos = (positions // ROW_LEN).astype(jnp.float32)
    col_pos = (positions % ROW_LEN).astype(jnp.float32)
    freq_index = jnp.arange(28, dtype=jnp.float32)
    frequency = jnp.power(jnp.float32(10000.0), -2.0 * freq_index / 56.0)
    angles = jnp.concatenate([jnp.zeros((positions.shape[0], 8), jnp.float32), row_pos[:, None] * frequency[None, :], col_pos[:, None] * frequency[None, :]], axis=1)
    return (jnp.cos(angles), jnp.sin(angles))

def rotate(vectors, cosine, sine_part):
    pairs = vectors.reshape(vectors.shape[0], vectors.shape[1], 64, 2)
    even_part = pairs[..., 0]
    odd_part = pairs[..., 1]
    cos_rows = cosine[:, None, :]
    sin_rows = sine_part[:, None, :]
    turned = jnp.stack([even_part * cos_rows - odd_part * sin_rows, even_part * sin_rows + odd_part * cos_rows], axis=-1)
    return turned.reshape(vectors.shape)

def head_norm(vectors, gain_row):
    mean_square = lax.optimization_barrier(jnp.mean(vectors * vectors, axis=-1, keepdims=True))
    return vectors * lax.rsqrt(mean_square + 1e-06) * gain_row

def reference(image_hidden, mod_table, step_index, qkv_weight, norm_gain, proj_weight, stale_kv, text_kv, patch_order):
    modulation = mod_table[step_index[0]]
    mod_shift = modulation[0]
    mod_scale = modulation[1]
    mod_gate = modulation[2]
    hidden = image_hidden.astype(jnp.float32)
    average = lax.optimization_barrier(jnp.mean(hidden, axis=-1, keepdims=True))
    variance = lax.optimization_barrier(jnp.mean((hidden - average) ** 2, axis=-1, keepdims=True))
    normed = (hidden - average) * lax.rsqrt(variance + 1e-06)
    modulated = ((1.0 + mod_scale) * normed + mod_shift).astype(jnp.bfloat16)
    projected_qkv = jnp.einsum('td,dcf->tcf', modulated.astype(jnp.float32), qkv_weight.astype(jnp.float32))
    positions = (patch_order[:, None] * TOK_DEV + jnp.arange(TOK_DEV, dtype=jnp.int32)[None, :]).reshape(-1).astype(jnp.int32)
    cosine, sine_part = rope_tables(positions)
    feat_all = HEADS * HEAD_DIM
    queries = rotate(head_norm(projected_qkv[:, 0].reshape(IMG, HEADS, HEAD_DIM), norm_gain[0]), cosine, sine_part).astype(jnp.bfloat16)
    fresh_keys = rotate(head_norm(projected_qkv[:, 1].reshape(IMG, HEADS, HEAD_DIM), norm_gain[1]), cosine, sine_part).astype(jnp.bfloat16)
    fresh_kv = jnp.stack([fresh_keys.reshape(IMG, feat_all), projected_qkv[:, 2].astype(jnp.bfloat16)])
    score_scale = 1.0 / jnp.sqrt(jnp.float32(HEAD_DIM))

    def one_block(device_block):
        first_row = (device_block * TOK_DEV).astype(jnp.int32)
        block_queries = lax.dynamic_slice_in_dim(queries, first_row, TOK_DEV, 0).astype(jnp.float32)
        own_mask = jnp.arange(IMG, dtype=jnp.int32) // TOK_DEV == device_block
        image_keys = jnp.where(own_mask[:, None], fresh_kv[0], stale_kv[0])
        image_values = jnp.where(own_mask[:, None], fresh_kv[1], stale_kv[1])
        all_keys = jnp.concatenate([text_kv[0], image_keys], axis=0).reshape(-1, HEADS, HEAD_DIM).astype(jnp.float32)
        all_values = jnp.concatenate([text_kv[1], image_values], axis=0).reshape(-1, HEADS, HEAD_DIM).astype(jnp.float32)
        scores = jnp.einsum('thd,khd->htk', block_queries, all_keys) * score_scale
        row_max = lax.optimization_barrier(jnp.max(scores, axis=-1, keepdims=True))
        exp_scores = jnp.exp(scores - row_max)
        row_sum = lax.optimization_barrier(jnp.sum(exp_scores, axis=-1))
        rounded = lax.optimization_barrier(exp_scores.astype(jnp.bfloat16)).astype(jnp.float32)
        attended = jnp.einsum('htk,khd->htd', rounded, all_values) / row_sum[..., None]
        return attended.astype(jnp.bfloat16).transpose(1, 0, 2).reshape(TOK_DEV, feat_all)
    attended = lax.map(one_block, jnp.arange(N_PATCH, dtype=jnp.int32)).reshape(IMG, feat_all)
    projected = jnp.dot(attended, proj_weight, preferred_element_type=jnp.float32)
    image_out = (hidden + mod_gate * projected).astype(jnp.bfloat16)
    return (image_out, fresh_kv)
```

```python
import functools

import jax
import jax.numpy as jnp
import numpy as np
from jax import lax
from jax.experimental import pallas as pl
from jax.experimental.pallas import tpu as pltpu
from jax.sharding import PartitionSpec as P

MESH = pl.DeviceIdType.MESH
TOK = 176
HALF = 1536
FEAT = 768
WIDE = 384
HD = 128
KEYS = 2944
KROWS = 3296
TEXT_ROW = 2816
LOG2E = 1.4426950408889634
SCORE = LOG2E / 128.0**0.5
CHUNKS = ((0, 96), (96, 80))
NT = (((1,), (1,)), ((), ()))


def stale_row(dz, dy, s):
    if dz == 0 and dy == 0:
        return jnp.where(s == 0, 2944, 176) if not isinstance(s, int) else (2944, 176)[s]
    if dz == 0:
        return 352 + ((dy - 1) * 2 + s) * TOK
    return 352 + (6 + dy * 2 + s) * TOK


def rows_at(start, n=TOK):
    if isinstance(start, int):
        return pl.ds(start, n)
    return pl.ds(pl.multiple_of(start, 16), n)


def lanes_at(start, n):
    if isinstance(start, int):
        return pl.ds(start, n)
    return pl.ds(pl.multiple_of(start, 128), n)


def kernel(
    hidden_ref, table_ref, step_ref, wqkv_ref, gain_ref, wproj_ref, stale_ref, text_ref, order_ref, freq_ref,
    out_ref, fresh_ref,
    w, wp, table, modv, hid, modded, qs, qb, kvb, fk, tx, tf, cost, sint,
    s1, s2, ob, orx, st, strx, psend, precv, pown, outb,
    lsem, hsend, hrecv, kvsend, kvrecv, fsem, fsend, tsend, trecv, qsend, qrecv,
    osend, orecv, stsend, strecv, prsend, prrecv,
):
    p = lax.axis_index("patch")
    h = lax.axis_index("head")
    x = p // 32
    y = (p // 8) % 4
    z = (p // 2) % 4
    c = p % 2
    zp = z + 1 - 2 * (z % 2)

    def dev(xx, yy, zz, cc):
        return (xx * 32 + yy * 8 + zz * 2 + cc, h)

    def ym(d):
        return (y + d) % 4

    partner = (p, 1 - h)
    other = dev(x, y, z, 1 - c)

    def kv_dev(dz, dy, cc):
        return dev(x, ym(dy), z if dz == 0 else zp, cc)

    def q_dev(r, cc):
        return dev(1 - x if r % 2 else x, y, (z + 2) % 4 if r // 2 else z, cc)

    def remote(src, dst, ss, rs, to):
        return pltpu.make_async_remote_copy(
            src_ref=src, dst_ref=dst, send_sem=ss, recv_sem=rs, device_id=to, device_id_type=MESH
        )

    own_cols = hid.at[h]
    loads = [
        pltpu.make_async_copy(hidden_ref, own_cols, lsem.at[0]),
        pltpu.make_async_copy(table_ref, table, lsem.at[1]),
        pltpu.make_async_copy(wqkv_ref.at[0], w.at[0], lsem.at[2]),
        pltpu.make_async_copy(wqkv_ref.at[1], w.at[1], lsem.at[3]),
        pltpu.make_async_copy(wqkv_ref.at[2], w.at[2], lsem.at[4]),
        pltpu.make_async_copy(wproj_ref, wp, lsem.at[5]),
    ]
    loads[0].start()
    loads[1].start()

    barrier = pltpu.get_barrier_semaphore()
    peers = [partner, other]
    for dz in range(2):
        for dy in range(4):
            if dz or dy:
                peers += [kv_dev(dz, dy, 0), kv_dev(dz, dy, 1)]
    for r in range(1, 4):
        peers += [q_dev(r, 0), q_dev(r, 1)]
    for peer in peers:
        pl.semaphore_signal(barrier, inc=1, device_id=peer, device_id_type=MESH)
    for load in loads[2:]:
        load.start()
    pl.semaphore_wait(barrier, len(peers))

    sends = []

    def go(copy):
        copy.start()
        sends.append(copy)

    hid_copies = []
    for i, (r0, n) in enumerate(CHUNKS):
        cp = remote(
            hidden_ref.at[pl.ds(r0, n)], hid.at[h, pl.ds(r0, n)], hsend.at[i], hrecv.at[i], partner
        )
        go(cp)
        hid_copies.append(cp)

    text_local = pltpu.make_async_copy(text_ref.at[:, lanes_at(c * WIDE, WIDE)], tx.at[c], trecv.at[c])
    text_local.start()
    go(remote(text_ref.at[:, lanes_at((1 - c) * WIDE, WIDE)], tx.at[c], tsend.at[0], trecv.at[c], other))
    for dz in range(2):
        for dy in range(4):
            if dz == 0 and dy == 0:
                continue
            slot = dz * 8 + ((4 - dy) % 4) * 2 + c
            for cc in range(2):
                go(
                    remote(
                        text_ref.at[:, pl.ds(cc * WIDE, WIDE)], tx.at[slot],
                        tsend.at[dz * 8 + dy * 2 + cc], trecv.at[slot], kv_dev(dz, dy, cc),
                    )
                )

    def kv_lanes(j):
        return lanes_at(j * HD, HD)

    kv_locals = []
    for j in range(3):
        cp = pltpu.make_async_copy(
            stale_ref.at[:, :, lanes_at(c * WIDE + j * HD, HD)],
            kvb.at[:, rows_at(stale_row(0, 0, c)), kv_lanes(j)],
            kvrecv.at[c, j],
        )
        cp.start()
        go(
            remote(
                stale_ref.at[:, :, lanes_at((1 - c) * WIDE + j * HD, HD)],
                kvb.at[:, rows_at(stale_row(0, 0, c)), kv_lanes(j)],
                kvsend.at[0, j], kvrecv.at[c, j], other,
            )
        )
        k = 1
        for dz, dy in ((1, 0), (0, 1), (0, 3)):
            back = (4 - dy) % 4
            for cc in range(2):
                go(
                    remote(
                        stale_ref.at[:, :, pl.ds(cc * WIDE + j * HD, HD)],
                        kvb.at[:, rows_at(stale_row(dz, back, c)), kv_lanes(j)],
                        kvsend.at[k, j], kvrecv.at[dz * 8 + back * 2 + c, j], kv_dev(dz, dy, cc),
                    )
                )
                k += 1

    def kv_wait(dz, dy, s, j):
        ref = kvb.at[:, rows_at(stale_row(dz, dy, s)), kv_lanes(j)]
        remote(ref, ref, kvsend.at[0, 0], kvrecv.at[dz * 8 + dy * 2 + s, j], other).wait_recv()

    block = order_ref[p]
    pos = lax.broadcasted_iota(jnp.int32, (TOK, HD), 0) + block * TOK
    row_pos = (pos >> 8).astype(jnp.float32)
    col_pos = (pos & 255).astype(jnp.float32)
    angles = row_pos * freq_ref[0:1, :] + col_pos * freq_ref[1:2, :]
    lane = lax.broadcasted_iota(jnp.int32, (TOK, HD), 1)
    even = (lane & 1) == 0
    cost[...] = jnp.cos(angles)
    sine = jnp.sin(angles)
    sint[...] = jnp.where(even, -sine, sine)

    loads[1].wait()
    step = step_ref[0]
    modv[0:1, :] = table[0, pl.ds(step, 1), :]
    modv[1:2, :] = 1.0 + table[1, pl.ds(step, 1), :]
    modv[2:3, :] = table[2, pl.ds(step, 1), :]

    def forward(j):
        k = 7
        for s in range(2):
            kv_wait(1, 0, s, j)
            src = kvb.at[:, rows_at(stale_row(1, 0, s)), kv_lanes(j)]
            for dy in (1, 3, 2):
                back = (4 - dy) % 4
                go(
                    remote(
                        src, kvb.at[:, rows_at(stale_row(1, back, s)), kv_lanes(j)],
                        kvsend.at[k, j], kvrecv.at[8 + back * 2 + s, j], kv_dev(0, dy, c),
                    )
                )
                k += 1
        for s, frm, to in ((0, 3, 1), (1, 1, 3)):
            kv_wait(0, frm, s, j)
            src = kvb.at[:, rows_at(stale_row(0, frm, s)), kv_lanes(j)]
            go(
                remote(
                    src, kvb.at[:, rows_at(stale_row(0, 2, s)), kv_lanes(j)],
                    kvsend.at[k, j], kvrecv.at[4 + s, j], kv_dev(0, to, c),
                )
            )
            k += 1

    for slot in range(16):
        remote(tx.at[slot], tx.at[slot], tsend.at[0], trecv.at[slot], other).wait_recv()
    for slot in range(16):
        both = tx[slot].astype(jnp.float32)
        tf[0, slot * 8 : slot * 8 + 8, :] = both[0:8]
        tf[1, slot * 8 : slot * 8 + 8, :] = both[8:16]
    kvb[0, TEXT_ROW : TEXT_ROW + 128, :] = tf[0].astype(jnp.bfloat16)
    kvb[1, TEXT_ROW : TEXT_ROW + 128, :] = tf[1].astype(jnp.bfloat16)

    forward(0)
    forward(1)
    forward(2)

    loads[0].wait()
    for i, (r0, n) in enumerate(CHUNKS):
        hid_copies[i].wait_recv()

        def norm_rows(g, _):
            rows = pl.ds(pl.multiple_of(r0 + g * 16, 16), 16)
            a = hid[0, rows, :].astype(jnp.float32)
            b = hid[1, rows, :].astype(jnp.float32)
            mean = (jnp.sum(a, axis=1, keepdims=True) + jnp.sum(b, axis=1, keepdims=True)) * (1.0 / 3072)
            a = a - mean
            b = b - mean
            var = (jnp.sum(a * a, axis=1, keepdims=True) + jnp.sum(b * b, axis=1, keepdims=True)) * (1.0 / 3072)
            inv = lax.rsqrt(var + 1e-6)
            modded[rows, 0:HALF] = (modv[1:2, 0:HALF] * (a * inv) + modv[0:1, 0:HALF]).astype(jnp.bfloat16)
            modded[rows, HALF:] = (modv[1:2, HALF:] * (b * inv) + modv[0:1, HALF:]).astype(jnp.bfloat16)
            return 0

        lax.fori_loop(0, n // 16, norm_rows, 0)

    def head_out(v, which):
        mean_square = jnp.mean(v * v, axis=1, keepdims=True)
        v = v * lax.rsqrt(mean_square + 1e-6) * gain_ref[which : which + 1, :]
        swapped = jnp.where(even, pltpu.roll(v, 127, 1), pltpu.roll(v, 1, 1))
        return (v * cost[...] + swapped * sint[...]).astype(jnp.bfloat16)

    for part in range(3):
        loads[2 + part].wait()
        for g2 in range(3):
            cols = pl.ds(g2 * 256, 256)
            acc = jnp.dot(modded[...], w[part, :, cols], preferred_element_type=jnp.float32)
            if part == 2:
                fk[1, :, cols] = acc.astype(jnp.bfloat16)
                continue
            for i in range(2):
                g = g2 * 2 + i
                res = head_out(acc[:, i * HD : (i + 1) * HD], part)
                if part == 1:
                    fk[0, :, g * HD : (g + 1) * HD] = res
                    continue
                qs[g] = res
                cc, j = g // 3, g % 3
                for r in range(1, 4):
                    go(remote(qs.at[g], qb.at[j, 2 * r + c], qsend.at[r, g], qrecv.at[j, 2 * r + c], q_dev(r, cc)))
        if part == 0:
            q_locals = []
            for j in range(3):
                pltpu.make_async_copy(qs.at[c * 3 + j], qb.at[j, c], qrecv.at[j, c]).start()
                go(remote(qs.at[(1 - c) * 3 + j], qb.at[j, c], qsend.at[0, j], qrecv.at[j, c], other))

    fresh_row = c * 3120
    pltpu.make_async_copy(
        fk.at[:, :, lanes_at(c * WIDE, WIDE)], kvb.at[:, rows_at(fresh_row), :], fsem.at[c]
    ).start()
    go(
        remote(
            fk.at[:, :, lanes_at((1 - c) * WIDE, WIDE)], kvb.at[:, rows_at(fresh_row), :],
            fsend.at[0], fsem.at[c], other,
        )
    )
    fresh_out = pltpu.make_async_copy(fk, fresh_ref, lsem.at[6])
    fresh_out.start()

    eye_a = lax.broadcasted_iota(jnp.int32, (128, 128), 0) == lax.broadcasted_iota(jnp.int32, (128, 128), 1)

    def q_wait(j, sub):
        remote(qb.at[j, sub], qb.at[j, sub], qsend.at[0, 0], qrecv.at[j, sub], other).wait_recv()

    def kv_wait_all(j):
        for dz in range(2):
            for dy in range(4):
                for s in range(2):
                    if (dz == 1 and dy == 0) or (dz == 0 and (dy, s) in ((3, 0), (1, 1))):
                        continue
                    kv_wait(dz, dy, s, j)

    def qk(j, r, s):
        lanes = kv_lanes(j)
        if r == 0:
            for u in range(2):
                s[u * TOK : (u + 1) * TOK, :] = lax.dot_general(
                    qb[j, u], kvb[0, pl.ds(352 * u, KEYS), lanes], NT, preferred_element_type=jnp.float32
                )
        else:
            q = qb[j, pl.ds(2 * r, 2)].reshape(2 * TOK, HD)
            s[...] = lax.dot_general(
                q, kvb[0, pl.ds(176, KEYS), lanes], NT, preferred_element_type=jnp.float32
            )

    ones = jnp.ones((KEYS, HD), jnp.bfloat16)

    def pv(j, r, s):
        lanes = kv_lanes(j)
        scores = s[...]
        top = jnp.max(scores, axis=1, keepdims=True) * SCORE
        e = jnp.exp2(scores * SCORE - top).astype(jnp.bfloat16)
        if r == 0:
            accs = []
            for u in range(2):
                vals = jnp.concatenate([kvb[1, pl.ds(352 * u, KEYS), lanes], ones], axis=1)
                accs.append(jnp.dot(e[u * TOK : (u + 1) * TOK], vals, preferred_element_type=jnp.float32))
        else:
            vals = jnp.concatenate([kvb[1, pl.ds(176, KEYS), lanes], ones], axis=1)
            acc = jnp.dot(e, vals, preferred_element_type=jnp.float32)
            accs = [acc[:TOK], acc[TOK:]]
        for u in range(2):
            acc = accs[u]
            total = acc[:, HD:]
            ob[j, 2 * r + u] = (acc[:, :HD] / total).astype(jnp.bfloat16)
            level = top[u * TOK : (u + 1) * TOK] + jnp.log2(total)
            st[2 * r + u, j, 0:1, :] = jnp.sum(jnp.where(eye_a, level[:128], 0.0), axis=0, keepdims=True)
            st[2 * r + u, j, 1:2, :] = jnp.sum(jnp.where(eye_a[:48], level[128:], 0.0), axis=0, keepdims=True)

    def o_copy(j, r, u):
        g = 3 * c + j
        return remote(ob.at[j, 2 * r + u], orx.at[g, r], osend.at[j, 2 * r + u], orecv.at[g, r], q_dev(r, u))

    def o_own(j):
        g = 3 * c + j
        local = pltpu.make_async_copy(ob.at[j, c], orx.at[g, 0], orecv.at[g, 0])
        far = remote(ob.at[j, 1 - c], orx.at[g, 0], osend.at[j, 0], orecv.at[g, 0], other)
        return local, far

    for s in range(2):
        remote(
            kvb.at[:, rows_at(s * 3120), :], kvb.at[:, rows_at(s * 3120), :], fsend.at[0], fsem.at[s], other
        ).wait_recv()
    kv_wait_all(0)
    q_wait(0, 0)
    q_wait(0, 1)
    qk(0, 0, s1)

    def head_step(j, last):
        for r in range(1, 4):
            q_wait(j, 2 * r)
            q_wait(j, 2 * r + 1)
            new, old = (s2, s1) if r % 2 else (s1, s2)
            qk(j, r, new)
            pv(j, r - 1, old)
            if r == 1:
                local, far = o_own(j)
                local.start()
                far.start()
            else:
                o_copy(j, r - 1, 0).start()
                o_copy(j, r - 1, 1).start()
        if not last:
            kv_wait_all(j + 1)
            q_wait(j + 1, 0)
            q_wait(j + 1, 1)
            qk(j + 1, 0, s1)
        pv(j, 3, s2)
        o_copy(j, 3, 0).start()
        o_copy(j, 3, 1).start()

    def loop_step(j, _):
        head_step(j, False)
        return 0

    lax.fori_loop(0, 2, loop_step, 0)
    head_step(2, True)

    pltpu.make_async_copy(st.at[c], strx.at[c, 0], strecv.at[c, 0]).start()
    go(remote(st.at[1 - c], strx.at[c, 0], stsend.at[0], strecv.at[c, 0], other))
    for r in range(1, 4):
        for u in range(2):
            go(remote(st.at[2 * r + u], strx.at[c, r], stsend.at[2 * r + u], strecv.at[c, r], q_dev(r, u)))

    for cc in range(2):
        for r in range(4):
            remote(strx.at[cc, r], strx.at[cc, r], stsend.at[0], strecv.at[cc, r], other).wait_recv()
    for g in range(6):
        for r in range(4):
            remote(orx.at[g, r], orx.at[g, r], osend.at[0, 0], orecv.at[g, r], other).wait_recv()
    for g in range(6):
        levels = [strx[g // 3, r, g % 3] for r in range(4)]
        most = jnp.maximum(jnp.maximum(levels[0], levels[1]), jnp.maximum(levels[2], levels[3]))
        weights = [jnp.exp2(v - most) for v in levels]
        total = weights[0] + weights[1] + weights[2] + weights[3]
        merged_a = jnp.zeros((128, HD), jnp.float32)
        merged_b = jnp.zeros((48, HD), jnp.float32)
        for r in range(4):
            share = weights[r] / total
            col_a = jnp.sum(jnp.where(eye_a, share[0:1], 0.0), axis=1, keepdims=True)
            col_b = jnp.sum(jnp.where(eye_a[:48], share[1:2], 0.0), axis=1, keepdims=True)
            part = orx[g, r].astype(jnp.float32)
            merged_a = merged_a + part[:128] * col_a
            merged_b = merged_b + part[128:] * col_b
        modded[0:128, g * HD : (g + 1) * HD] = merged_a.astype(jnp.bfloat16)
        modded[128:176, g * HD : (g + 1) * HD] = merged_b.astype(jnp.bfloat16)

    loads[5].wait()
    pcopies = []
    for i in range(3):
        part = jnp.dot(
            modded[:, 0:FEAT], wp[:, lanes_at((1 - h) * HALF + i * 512, 512)], preferred_element_type=jnp.float32
        )
        cols = pl.ds(i * 512, 512)
        psend[:, cols] = part.astype(jnp.bfloat16)
        cp = remote(psend.at[:, cols], precv.at[:, cols], prsend.at[i], prrecv.at[i], partner)
        go(cp)
        pcopies.append(cp)
    for i in range(3):
        pown[:, i * 512 : (i + 1) * 512] = jnp.dot(
            modded[:, 0:FEAT], wp[:, lanes_at(h * HALF + i * 512, 512)], preferred_element_type=jnp.float32
        )
    out_copies = []
    for i in range(3):
        pcopies[i].wait_recv()
        cols = slice(i * 512, (i + 1) * 512)
        gate = modv[2:3, lanes_at(h * HALF + i * 512, 512)]
        summed = pown[:, cols] + precv[:, cols].astype(jnp.float32)
        outb[:, cols] = (hid[h, :, cols].astype(jnp.float32) + gate * summed).astype(jnp.bfloat16)
        cp = pltpu.make_async_copy(
            outb.at[:, pl.ds(i * 512, 512)], out_ref.at[:, pl.ds(i * 512, 512)], lsem.at[7 + i]
        )
        cp.start()
        out_copies.append(cp)

    for cp in sends:
        cp.wait_send()
    for j in range(3):
        o_own(j)[1].wait_send()
        for r in range(1, 4):
            o_copy(j, r, 0).wait_send()
            o_copy(j, r, 1).wait_send()
    fresh_out.wait()
    for cp in out_copies:
        cp.wait()


def frequencies():
    freq = np.power(10000.0, -2.0 * np.arange(28) / 56.0).astype(np.float32)
    both = np.zeros((2, 64), np.float32)
    both[0, 8:36] = freq
    both[1, 36:64] = freq
    return np.repeat(both, 2, axis=1)


def body(
    image_hidden, mod_table, step_index, qkv_weight, norm_gain, proj_weight, stale_kv, text_kv, patch_order
):
    bf, f32 = jnp.bfloat16, jnp.float32
    anywhere = pl.BlockSpec(memory_space=pl.ANY)
    vmem = pl.BlockSpec(memory_space=pltpu.VMEM)
    smem = pl.BlockSpec(memory_space=pltpu.SMEM)
    V = pltpu.VMEM
    S = pltpu.SemaphoreType.DMA
    scratch = [
        V((3, 3072, FEAT), bf),
        V((FEAT, 3072), bf),
        V((3, 28, 3072), f32),
        V((8, 3072), f32),
        V((2, TOK, HALF), bf),
        V((TOK, 3072), bf),
        V((6, TOK, HD), bf),
        V((3, 8, TOK, HD), bf),
        V((2, KROWS, WIDE), bf),
        V((2, TOK, FEAT), bf),
        V((16, 16, WIDE), bf),
        V((2, 128, WIDE), f32),
        V((TOK, HD), f32),
        V((TOK, HD), f32),
        V((2 * TOK, KEYS), f32),
        V((2 * TOK, KEYS), f32),
        V((3, 8, TOK, HD), bf),
        V((6, 4, TOK, HD), bf),
        V((8, 3, 8, 128), f32),
        V((2, 4, 3, 8, 128), f32),
        V((TOK, HALF), bf),
        V((TOK, HALF), bf),
        V((TOK, HALF), f32),
        V((TOK, HALF), bf),
        S((10,)),
        S((2,)), S((2,)),
        S((15, 3)), S((16, 3)),
        S((2,)), S((1,)),
        S((16,)), S((16,)),
        S((4, 6)), S((3, 8)),
        S((3, 8)), S((6, 4)),
        S((8,)), S((2, 4)),
        S((3,)), S((3,)),
    ]
    call = pl.pallas_call(
        kernel,
        out_shape=(
            jax.ShapeDtypeStruct((TOK, HALF), bf),
            jax.ShapeDtypeStruct((2, TOK, FEAT), bf),
        ),
        in_specs=[
            anywhere, anywhere, smem, anywhere, vmem, anywhere, anywhere, anywhere, smem, vmem,
        ],
        out_specs=(anywhere, anywhere),
        scratch_shapes=scratch,
        compiler_params=pltpu.CompilerParams(
            collective_id=0, has_side_effects=True, vmem_limit_bytes=58 * 2**20
        ),
        cost_estimate=pl.CostEstimate(flops=10**10, bytes_accessed=2 * 10**7, transcendentals=13 * 10**6),
    )
    return call(
        image_hidden,
        jnp.transpose(mod_table, (1, 0, 2)),
        step_index,
        jnp.transpose(qkv_weight, (1, 0, 2)),
        norm_gain,
        proj_weight,
        stale_kv,
        text_kv.reshape(16, FEAT),
        patch_order,
        jnp.asarray(frequencies()),
    )


def solution(mesh):
    return jax.shard_map(
        body,
        mesh=mesh,
        in_specs=(
            P("patch", "head"),
            P(),
            P(),
            P(None, None, "head"),
            P(),
            P("head", None),
            P(None, "patch", "head"),
            P(None, "patch", "head"),
            P(),
        ),
        out_specs=(P("patch", "head"), P(None, "patch", "head")),
        check_vma=False,
    )
```

```python
import functools

import jax
import jax.numpy as jnp
import numpy as np
from jax import lax
from jax.experimental import pallas as pl
from jax.experimental.pallas import tpu as pltpu
from jax.sharding import PartitionSpec as P

MESH = pl.DeviceIdType.MESH
TOK = 176
BLK = 192
LIVE = 184
HALF = 1536
FEAT = 768
WIDE = 384
HD = 128
KEYS = 16 * BLK
KROWS = 18 * BLK
PIECE = 96
LOG2E = 1.4426950408889634
SCORE = LOG2E / 128.0**0.5
CHUNKS = ((0, 48), (48, 48), (96, 48), (144, 32))
NT = (((1,), (1,)), ((), ()))


def stale_row(dz, dy, s):
    if dz == 0 and dy == 0:
        return jnp.where(s == 0, 16 * BLK, BLK) if not isinstance(s, int) else (16 * BLK, BLK)[s]
    if dz == 0:
        return (2 + (dy - 1) * 2 + s) * BLK
    return (8 + dy * 2 + s) * BLK


def rows_at(start, n=BLK):
    if isinstance(start, int):
        return pl.ds(start, n)
    return pl.ds(pl.multiple_of(start, 16), n)


def lanes_at(start, n):
    if isinstance(start, int):
        return pl.ds(start, n)
    return pl.ds(pl.multiple_of(start, 128), n)


def kernel(
    hidden_ref, table_ref, step_ref, wqkv_ref, gain_ref, wproj_ref, stale_ref, text_ref, order_ref, freq_ref,
    out_ref, fresh_ref,
    w, wp, wo, table, modv, hid, modded, qs, qb, kvb, stg, txs, fk, mask, cost, sint,
    s1, s2, ob, orx, att, pown, outb,
    lsem, hsend, hrecv, kvsend, kvrecv, fsem, fsend, qsend, qrecv,
    osend, orecv, wsend, wrecv, asend, arecv,
):
    p = lax.axis_index("patch")
    h = lax.axis_index("head")
    x = p // 32
    y = (p // 8) % 4
    z = (p // 2) % 4
    c = p % 2
    zk = z + 1 - 2 * (z % 2)
    zq = (z + 3 + 2 * (z % 2)) % 4

    def dev(xx, yy, zz, cc):
        return (xx * 32 + yy * 8 + zz * 2 + cc, h)

    partner = (p, 1 - h)
    other = dev(x, y, z, 1 - c)
    beside = ((1 - x) * 32 + y * 8 + z * 2 + c, 1 - h)

    def kv_dev(dz, dy, cc):
        return dev(x, (y + dy) % 4, zk if dz else z, cc)

    def q_dev(r, cc):
        return dev(1 - x if r % 2 else x, y, zq if r // 2 else z, cc)

    def remote(src, dst, ss, rs, to):
        return pltpu.make_async_remote_copy(
            src_ref=src, dst_ref=dst, send_sem=ss, recv_sem=rs, device_id=to, device_id_type=MESH
        )

    loads = [
        pltpu.make_async_copy(hidden_ref, hid.at[h], lsem.at[0]),
        pltpu.make_async_copy(table_ref, table, lsem.at[1]),
        pltpu.make_async_copy(wqkv_ref.at[0], w.at[0], lsem.at[2]),
        pltpu.make_async_copy(wqkv_ref.at[1], w.at[1], lsem.at[3]),
        pltpu.make_async_copy(wqkv_ref.at[2], w.at[2], lsem.at[4]),
        pltpu.make_async_copy(wproj_ref.at[:, lanes_at(h * HALF, HALF)], wp, lsem.at[5]),
        pltpu.make_async_copy(stale_ref, stg.at[:, pl.ds(0, TOK)], lsem.at[6]),
        pltpu.make_async_copy(text_ref, txs, lsem.at[7]),
    ]
    for i in (6, 7, 0, 1):
        loads[i].start()

    barrier = pltpu.get_barrier_semaphore()
    peers = [partner, other, beside, kv_dev(0, 2, c)]
    for dz, dy in ((1, 0), (0, 1), (0, 3)):
        peers += [kv_dev(dz, dy, 0), kv_dev(dz, dy, 1)]
    for r in range(1, 4):
        peers += [q_dev(r, 0), q_dev(r, 1)]
    for peer in peers:
        pl.semaphore_signal(barrier, inc=1, device_id=peer, device_id_type=MESH)
    for i in (2, 3, 4, 5):
        loads[i].start()

    loads[6].wait()
    loads[7].wait()
    words = txs[...].astype(jnp.float32)
    key_tail = jnp.concatenate([words[0:8], words[0:8]], axis=0).astype(jnp.bfloat16)
    value_tail = jnp.concatenate([words[8:16], jnp.zeros((8, FEAT), jnp.float32)], axis=0).astype(jnp.bfloat16)
    stg[0, TOK:BLK, :] = key_tail
    stg[1, TOK:BLK, :] = value_tail
    fk[0, TOK:BLK, :] = key_tail
    fk[1, TOK:BLK, :] = value_tail

    pl.semaphore_wait(barrier, len(peers))

    sends = []

    def go(copy):
        copy.start()
        sends.append(copy)
        return copy

    hid_copies = [
        remote(hidden_ref.at[pl.ds(r0, n)], hid.at[h, pl.ds(r0, n)], hsend.at[i], hrecv.at[i], partner)
        for i, (r0, n) in enumerate(CHUNKS)
    ]
    hid_copies[0].start()
    hid_copies[1].start()

    def hid_next(i):
        hid_copies[i - 2].wait_send()
        go(hid_copies[i])

    def kv_lanes(j):
        return pl.ds(j * HD, HD)

    def own_blocks(j):
        rows = rows_at(stale_row(0, 0, c))
        pltpu.make_async_copy(
            stg.at[:, :, lanes_at(c * WIDE + j * HD, HD)], kvb.at[:, rows, kv_lanes(j)], kvrecv.at[c, j]
        ).start()
        k = 1
        for dz, dy in ((1, 0), (0, 1), (0, 3)):
            back = (4 - dy) % 4
            for cc in range(2):
                go(
                    remote(
                        stg.at[:, :, pl.ds(cc * WIDE + j * HD, HD)],
                        kvb.at[:, rows_at(stale_row(dz, back, c)), kv_lanes(j)],
                        kvsend.at[k, j], kvrecv.at[dz * 8 + back * 2 + c, j], kv_dev(dz, dy, cc),
                    )
                )
                k += 1
        go(
            remote(
                stg.at[:, :, lanes_at((1 - c) * WIDE + j * HD, HD)], kvb.at[:, rows, kv_lanes(j)],
                kvsend.at[0, j], kvrecv.at[c, j], other,
            )
        )

    def kv_wait(dz, dy, s, j):
        ref = kvb.at[:, rows_at(stale_row(dz, dy, s)), kv_lanes(j)]
        remote(ref, ref, kvsend.at[0, 0], kvrecv.at[dz * 8 + dy * 2 + s, j], other).wait_recv()

    def forward_y(j):
        k = 7
        for s in range(2):
            kv_wait(1, 0, s, j)
            src = kvb.at[:, rows_at(stale_row(1, 0, s)), kv_lanes(j)]
            for dy in (1, 3):
                back = (4 - dy) % 4
                go(
                    remote(
                        src, kvb.at[:, rows_at(stale_row(1, back, s)), kv_lanes(j)],
                        kvsend.at[k, j], kvrecv.at[8 + back * 2 + s, j], kv_dev(0, dy, c),
                    )
                )
                k += 1
        for s, frm, to in ((0, 3, 1), (1, 1, 3)):
            kv_wait(0, frm, s, j)
            src = kvb.at[:, rows_at(stale_row(0, frm, s)), kv_lanes(j)]
            go(
                remote(
                    src, kvb.at[:, rows_at(stale_row(0, 2, s)), kv_lanes(j)],
                    kvsend.at[k, j], kvrecv.at[4 + s, j], kv_dev(0, to, c),
                )
            )
            k += 1

    def forward_z(j):
        for s in range(2):
            kv_wait(0, 2, s, j)
            go(
                remote(
                    kvb.at[:, rows_at(stale_row(0, 2, s)), kv_lanes(j)],
                    kvb.at[:, rows_at(stale_row(1, 2, s)), kv_lanes(j)],
                    kvsend.at[13 + s, j], kvrecv.at[12 + s, j], kv_dev(1, 0, c),
                )
            )

    own_blocks(0)

    block = order_ref[p]
    pos = lax.broadcasted_iota(jnp.int32, (TOK, HD), 0) + block * TOK
    row_pos = (pos >> 8).astype(jnp.float32)
    col_pos = (pos & 255).astype(jnp.float32)
    angles = row_pos * freq_ref[0:1, :] + col_pos * freq_ref[1:2, :]
    lane = lax.broadcasted_iota(jnp.int32, (TOK, HD), 1)
    even = (lane & 1) == 0
    cost[...] = jnp.cos(angles)
    sine = jnp.sin(angles)
    sint[...] = jnp.where(even, -sine, sine)

    live = lax.broadcasted_iota(jnp.int32, (BLK, HD), 0) < LIVE
    for i in range(16):
        mask[i * BLK : (i + 1) * BLK, :] = jnp.where(live, 1.0, 0.0).astype(jnp.bfloat16)

    loads[1].wait()
    step = step_ref[0]
    modv[0:1, :] = table[0, pl.ds(step, 1), :]
    modv[1:2, :] = 1.0 + table[1, pl.ds(step, 1), :]
    modv[2:3, :] = table[2, pl.ds(step, 1), :]

    loads[0].wait()

    def layer_norm(i):
        r0, n = CHUNKS[i]
        hid_copies[i].wait_recv()

        rows = pl.ds(r0, n)
        a = hid[0, rows, :].astype(jnp.float32)
        b = hid[1, rows, :].astype(jnp.float32)
        mean = (jnp.sum(a, axis=1, keepdims=True) + jnp.sum(b, axis=1, keepdims=True)) * (1.0 / 3072)
        a = a - mean
        b = b - mean
        var = (jnp.sum(a * a, axis=1, keepdims=True) + jnp.sum(b * b, axis=1, keepdims=True)) * (1.0 / 3072)
        inv = lax.rsqrt(var + 1e-6)
        modded[rows, 0:HALF] = (modv[1:2, 0:HALF] * (a * inv) + modv[0:1, 0:HALF]).astype(jnp.bfloat16)
        modded[rows, HALF:] = (modv[1:2, HALF:] * (b * inv) + modv[0:1, HALF:]).astype(jnp.bfloat16)

    forward_y(0)
    own_blocks(1)
    hid_next(2)
    layer_norm(0)
    forward_y(1)
    own_blocks(2)
    hid_next(3)
    layer_norm(1)
    layer_norm(2)
    forward_y(2)
    layer_norm(3)

    mine = pl.ds(pl.multiple_of(c * WIDE + y * PIECE, 16), PIECE)
    go(
        remote(
            wproj_ref.at[mine, lanes_at((1 - h) * HALF, HALF)], wo.at[mine], wsend.at[0], wrecv.at[y], beside
        )
    )

    def piece_wait(d):
        yy = (y + d) % 4
        ref = wo.at[pl.ds(pl.multiple_of(c * WIDE + yy * PIECE, 16), PIECE)]
        remote(ref, ref, wsend.at[0], wrecv.at[yy], other).wait_recv()

    def head_out(v, which):
        mean_square = jnp.mean(v * v, axis=1, keepdims=True)
        v = v * lax.rsqrt(mean_square + 1e-6) * gain_ref[which : which + 1, :]
        swapped = jnp.where(even, pltpu.roll(v, 127, 1), pltpu.roll(v, 1, 1))
        return (v * cost[...] + swapped * sint[...]).astype(jnp.bfloat16)

    def send_queries(j):
        for r in (1, 2, 3):
            for cc in range(2):
                g = cc * 3 + j
                go(remote(qs.at[g], qb.at[j, 2 * r + c], qsend.at[r, g], qrecv.at[j, 2 * r + c], q_dev(r, cc)))
        pltpu.make_async_copy(qs.at[c * 3 + j], qb.at[j, c], qrecv.at[j, c]).start()
        go(remote(qs.at[(1 - c) * 3 + j], qb.at[j, c], qsend.at[0, j], qrecv.at[j, c], other))

    for part in range(3):
        loads[2 + part].wait()
        for g2 in range(3):
            cols = pl.ds(g2 * 256, 256)
            acc = jnp.dot(modded[...], w[part, :, cols], preferred_element_type=jnp.float32)
            if part == 2:
                fk[1, 0:TOK, cols] = acc.astype(jnp.bfloat16)
                continue
            for i in range(2):
                g = g2 * 2 + i
                res = head_out(acc[:, i * HD : (i + 1) * HD], part)
                if part == 1:
                    fk[0, 0:TOK, g * HD : (g + 1) * HD] = res
                    continue
                qs[g] = res
        if part == 0:
            send_queries(0)
            forward_z(0)
    send_queries(1)

    fresh_row = rows_at(c * (17 * BLK))
    pltpu.make_async_copy(fk.at[:, :, lanes_at(c * WIDE, WIDE)], kvb.at[:, fresh_row, :], fsem.at[c]).start()
    go(
        remote(
            fk.at[:, :, lanes_at((1 - c) * WIDE, WIDE)], kvb.at[:, fresh_row, :], fsend.at[0], fsem.at[c], other
        )
    )
    fresh_out = pltpu.make_async_copy(fk.at[:, pl.ds(0, TOK)], fresh_ref, lsem.at[8])
    fresh_out.start()

    eye = lax.broadcasted_iota(jnp.int32, (128, 128), 0) == lax.broadcasted_iota(jnp.int32, (128, 128), 1)

    def q_wait(j, sub):
        remote(qb.at[j, sub], qb.at[j, sub], qsend.at[0, 0], qrecv.at[j, sub], other).wait_recv()

    def kv_wait_all(j):
        for dz in range(2):
            for dy in range(4):
                for s in range(2):
                    if (dz == 1 and dy == 0) or (dz == 0 and (dy == 2 or (dy, s) in ((3, 0), (1, 1)))):
                        continue
                    kv_wait(dz, dy, s, j)

    def qk(j, r, s):
        if r == 0:
            for u in range(2):
                s[u * TOK : (u + 1) * TOK, :] = lax.dot_general(
                    qb[j, u], kvb[0, pl.ds(2 * BLK * u, KEYS), kv_lanes(j)], NT,
                    preferred_element_type=jnp.float32,
                )
        else:
            q = qb[j, 2 * r : 2 * r + 2].reshape(2 * TOK, HD)
            s[...] = lax.dot_general(
                q, kvb[0, pl.ds(BLK, KEYS), kv_lanes(j)], NT, preferred_element_type=jnp.float32
            )

    def pv(j, r, s):
        scores = s[...]
        top = jnp.max(scores, axis=1, keepdims=True) * SCORE
        e = jnp.exp2(scores * SCORE - top).astype(jnp.bfloat16)
        if r == 0:
            accs = []
            for u in range(2):
                vals = jnp.concatenate([kvb[1, pl.ds(2 * BLK * u, KEYS), kv_lanes(j)], mask[...]], axis=1)
                accs.append(jnp.dot(e[u * TOK : (u + 1) * TOK], vals, preferred_element_type=jnp.float32))
        else:
            vals = jnp.concatenate([kvb[1, pl.ds(BLK, KEYS), kv_lanes(j)], mask[...]], axis=1)
            acc = jnp.dot(e, vals, preferred_element_type=jnp.float32)
            accs = [acc[:TOK], acc[TOK:]]
        for u in range(2):
            acc = accs[u]
            total = acc[:, HD:]
            ob[j, 2 * r + u, 0:TOK, :] = (acc[:, :HD] / total).astype(jnp.bfloat16)
            level = top[u * TOK : (u + 1) * TOK] + jnp.log2(total)
            la = jnp.sum(jnp.where(eye, level[:128], 0.0), axis=0, keepdims=True)
            lb = jnp.sum(jnp.where(eye[:48], level[128:], 0.0), axis=0, keepdims=True)
            rest = jnp.concatenate([la, lb], axis=0)
            terms = []
            for _ in range(3):
                term = rest.astype(jnp.bfloat16).astype(jnp.float32)
                terms.append(term)
                rest = rest - term
            terms.append(jnp.zeros((10, HD), jnp.float32))
            ob[j, 2 * r + u, TOK:BLK, :] = jnp.concatenate(terms, axis=0).astype(jnp.bfloat16)

    def o_copy(j, r, u):
        g = 3 * c + j
        return remote(ob.at[j, 2 * r + u], orx.at[g, r], osend.at[j, 2 * r + u], orecv.at[g, r], q_dev(r, u))

    def o_send(j, r):
        if r == 0:
            g = 3 * c + j
            pltpu.make_async_copy(ob.at[j, c], orx.at[g, 0], orecv.at[g, 0]).start()
            go(remote(ob.at[j, 1 - c], orx.at[g, 0], osend.at[j, 0], orecv.at[g, 0], other))
        else:
            go(o_copy(j, r, 0))
            go(o_copy(j, r, 1))

    att_copies = []

    def merge(j):
        for cc in range(2):
            for r in range(4):
                g = 3 * cc + j
                remote(orx.at[g, r], orx.at[g, r], osend.at[0, 0], orecv.at[g, r], other).wait_recv()
        for cc in range(2):
            g = 3 * cc + j
            levels = []
            for r in range(4):
                tail = orx[g, r, TOK:BLK, :].astype(jnp.float32)
                levels.append(tail[0:2] + tail[2:4] + tail[4:6])
            most = jnp.maximum(jnp.maximum(levels[0], levels[1]), jnp.maximum(levels[2], levels[3]))
            weights = [jnp.exp2(v - most) for v in levels]
            total = weights[0] + weights[1] + weights[2] + weights[3]
            merged_a = jnp.zeros((128, HD), jnp.float32)
            merged_b = jnp.zeros((48, HD), jnp.float32)
            for r in range(4):
                share = weights[r] / total
                col_a = jnp.sum(jnp.where(eye, share[0:1], 0.0), axis=1, keepdims=True)
                col_b = jnp.sum(jnp.where(eye[:48], share[1:2], 0.0), axis=1, keepdims=True)
                part = orx[g, r, 0:TOK, :].astype(jnp.float32)
                merged_a = merged_a + part[:128] * col_a
                merged_b = merged_b + part[128:] * col_b
            att[h, j, 0:128, cc * HD : (cc + 1) * HD] = merged_a.astype(jnp.bfloat16)
            att[h, j, 128:TOK, cc * HD : (cc + 1) * HD] = merged_b.astype(jnp.bfloat16)
        att_copies.append(go(remote(att.at[h, j], att.at[h, j], asend.at[j], arecv.at[j], partner)))

    for s in range(2):
        ref = kvb.at[:, pl.ds(s * 17 * BLK, BLK), :]
        remote(ref, ref, fsend.at[0], fsem.at[s], other).wait_recv()
    units = [(0, r) for r in (0, 1, 2, 3)] + [(1, r) for r in (0, 1, 2, 3)] + [(2, r) for r in (1, 2, 3, 0)]

    def score(i):
        j, r = units[i]
        if i % 4 == 0:
            kv_wait_all(j)
        q_wait(j, 2 * r)
        q_wait(j, 2 * r + 1)
        qk(j, r, s2 if i % 2 else s1)

    score(0)
    for i in range(12):
        if i < 11:
            score(i + 1)
        pv(*units[i], s2 if i % 2 else s1)
        o_send(*units[i])
        if i == 0:
            send_queries(2)
            forward_z(1)
        elif i == 3:
            forward_z(2)
            piece_wait(0)
        elif i == 5:
            for d in (1, 3, 2):
                go(remote(wo.at[mine], wo.at[mine], wsend.at[d], wrecv.at[y], kv_dev(0, d, c)))
        elif i == 6:
            merge(0)
        elif i == 10:
            merge(1)
    for d in (1, 3, 2):
        piece_wait(d)
    half = wo.at[rows_at(c * WIDE, WIDE)]
    go(remote(half, half, wsend.at[4], wrecv.at[4], other))
    merge(2)

    loads[5].wait()
    half = wo.at[rows_at((1 - c) * WIDE, WIDE)]
    remote(half, half, wsend.at[4], wrecv.at[4], other).wait_recv()

    def rows_of(weights, j, cols):
        return jnp.concatenate(
            [weights[j * HD : (j + 1) * HD, cols], weights[WIDE + j * HD : WIDE + (j + 1) * HD, cols]], axis=0
        )

    att_copies[0].wait_recv()
    att_copies[1].wait_recv()
    for i in range(3):
        cols = pl.ds(i * 512, 512)
        acc = None
        for grp, weights, count in ((h, wp, 3), (1 - h, wo, 2)):
            for j in range(count):
                term = jnp.dot(att[grp, j], rows_of(weights, j, cols), preferred_element_type=jnp.float32)
                acc = term if acc is None else acc + term
        pown[:, cols] = acc
    att_copies[2].wait_recv()
    out_copies = []
    for i in range(3):
        cols = pl.ds(i * 512, 512)
        gate = modv[2:3, lanes_at(h * HALF + i * 512, 512)]
        summed = pown[:, cols] + jnp.dot(att[1 - h, 2], rows_of(wo, 2, cols), preferred_element_type=jnp.float32)
        outb[:, cols] = (hid[h, :, cols].astype(jnp.float32) + gate * summed).astype(jnp.bfloat16)
        cp = pltpu.make_async_copy(outb.at[:, cols], out_ref.at[:, cols], lsem.at[9 + i])
        cp.start()
        out_copies.append(cp)

    for cp in sends:
        cp.wait_send()
    fresh_out.wait()
    for cp in out_copies:
        cp.wait()


def copy_kernel(a_ref, b_ref, c_ref, d_ref, a, b, sem):
    pairs = [
        (a_ref.at[pl.ds(r, n)], a.at[pl.ds(r, n)], c_ref.at[pl.ds(r, n)]) for r, n in ((0, 96), (96, 80))
    ]
    pairs += [(b_ref.at[i], b.at[i], d_ref.at[i]) for i in range(2)]
    ins = [pltpu.make_async_copy(src, mid, sem.at[i]) for i, (src, mid, _) in enumerate(pairs)]
    outs = [pltpu.make_async_copy(mid, dst, sem.at[4 + i]) for i, (_, mid, dst) in enumerate(pairs)]
    for cp in ins:
        cp.start()
    for cp_in, cp_out in zip(ins, outs):
        cp_in.wait()
        cp_out.start()
    for cp in outs:
        cp.wait()


def frequencies():
    freq = np.power(10000.0, -2.0 * np.arange(28) / 56.0).astype(np.float32)
    both = np.zeros((2, 64), np.float32)
    both[0, 8:36] = freq
    both[1, 36:64] = freq
    return np.repeat(both, 2, axis=1)


def body(
    image_hidden, mod_table, step_index, qkv_weight, norm_gain, proj_weight, stale_kv, text_kv, patch_order
):
    bf, f32 = jnp.bfloat16, jnp.float32
    anywhere = pl.BlockSpec(memory_space=pl.ANY)
    vmem = pl.BlockSpec(memory_space=pltpu.VMEM)
    smem = pl.BlockSpec(memory_space=pltpu.SMEM)
    V = pltpu.VMEM
    S = pltpu.SemaphoreType.DMA
    scratch = [
        V((3, 3072, FEAT), bf),
        V((FEAT, HALF), bf),
        V((FEAT, HALF), bf),
        V((3, 28, 3072), f32),
        V((8, 3072), f32),
        V((2, TOK, HALF), bf),
        V((TOK, 3072), bf),
        V((6, TOK, HD), bf),
        V((3, 8, TOK, HD), bf),
        V((2, KROWS, WIDE), bf),
        V((2, BLK, FEAT), bf),
        V((16, FEAT), bf),
        V((2, BLK, FEAT), bf),
        V((KEYS, HD), bf),
        V((TOK, HD), f32),
        V((TOK, HD), f32),
        V((2 * TOK, KEYS), f32),
        V((2 * TOK, KEYS), f32),
        V((3, 8, BLK, HD), bf),
        V((6, 4, BLK, HD), bf),
        V((2, 3, TOK, 2 * HD), bf),
        V((TOK, HALF), f32),
        V((TOK, HALF), bf),
        S((12,)),
        S((4,)), S((4,)),
        S((15, 3)), S((16, 3)),
        S((2,)), S((1,)),
        S((4, 6)), S((3, 8)),
        S((3, 8)), S((6, 4)),
        S((5,)), S((5,)),
        S((3,)), S((3,)),
    ]
    call = pl.pallas_call(
        kernel,
        out_shape=(
            jax.ShapeDtypeStruct((TOK, HALF), bf),
            jax.ShapeDtypeStruct((2, TOK, FEAT), bf),
        ),
        in_specs=[
            anywhere, anywhere, smem, anywhere, vmem, anywhere, anywhere, anywhere, smem, vmem,
        ],
        out_specs=(anywhere, anywhere),
        scratch_shapes=scratch,
        compiler_params=pltpu.CompilerParams(
            collective_id=0, has_side_effects=True, vmem_limit_bytes=58 * 2**20
        ),
        cost_estimate=pl.CostEstimate(flops=10**10, bytes_accessed=2 * 10**7, transcendentals=13 * 10**6),
    )
    image_out, fresh_kv = call(
        image_hidden,
        jnp.transpose(mod_table, (1, 0, 2)),
        step_index,
        jnp.transpose(qkv_weight, (1, 0, 2)),
        norm_gain,
        proj_weight,
        stale_kv,
        text_kv.reshape(16, FEAT),
        patch_order,
        jnp.asarray(frequencies()),
    )
    return pl.pallas_call(
        copy_kernel,
        out_shape=(
            jax.ShapeDtypeStruct((TOK, HALF), bf),
            jax.ShapeDtypeStruct((2, TOK, FEAT), bf),
        ),
        in_specs=[anywhere, anywhere],
        out_specs=(anywhere, anywhere),
        scratch_shapes=[V((TOK, HALF), bf), V((2, TOK, FEAT), bf), S((8,))],
        compiler_params=pltpu.CompilerParams(vmem_limit_bytes=58 * 2**20),
    )(image_out, fresh_kv)


def solution(mesh):
    return jax.shard_map(
        body,
        mesh=mesh,
        in_specs=(
            P("patch", "head"),
            P(),
            P(),
            P(None, None, "head"),
            P(),
            P("head", None),
            P(None, "patch", "head"),
            P(None, "patch", "head"),
            P(),
        ),
        out_specs=(P("patch", "head"), P(None, "patch", "head")),
        check_vma=False,
    )
```

```python
import functools

import jax
import jax.numpy as jnp
import numpy as np
from jax import lax
from jax.experimental import pallas as pl
from jax.experimental.pallas import tpu as pltpu
from jax.sharding import PartitionSpec as P

MESH = pl.DeviceIdType.MESH
TOK = 176
BLK = 192
LIVE = 184
HALF = 1536
FEAT = 768
WIDE = 384
HD = 128
KEYS = 16 * BLK
KROWS = 18 * BLK
PIECE = 96
LOG2E = 1.4426950408889634
SCORE = LOG2E / 128.0**0.5
CHUNKS = ((0, 48), (48, 48), (96, 48), (144, 32))
NT = (((1,), (1,)), ((), ()))


def stale_row(dz, dy, s):
    if dz == 0 and dy == 0:
        return jnp.where(s == 0, 16 * BLK, BLK) if not isinstance(s, int) else (16 * BLK, BLK)[s]
    if dz == 0:
        return (2 + (dy - 1) * 2 + s) * BLK
    return (8 + dy * 2 + s) * BLK


def rows_at(start, n=BLK):
    if isinstance(start, int):
        return pl.ds(start, n)
    return pl.ds(pl.multiple_of(start, 16), n)


def lanes_at(start, n):
    if isinstance(start, int):
        return pl.ds(start, n)
    return pl.ds(pl.multiple_of(start, 128), n)


def kernel(
    hidden_ref, table_ref, step_ref, wqkv_ref, gain_ref, wproj_ref, stale_ref, text_ref, order_ref, freq_ref,
    out_ref, fresh_ref,
    w, wp, wo, table, modv, hid, modded, qs, qb, kvb, stg, txs, fk, mask, cost, sint,
    s1, s2, ob, orx, att, pown, outb,
    lsem, hsend, hrecv, kvsend, kvrecv, fsem, fsend, qsend, qrecv,
    osend, orecv, wsend, wrecv, asend, arecv,
):
    p = lax.axis_index("patch")
    h = lax.axis_index("head")
    x = p // 32
    y = (p // 8) % 4
    z = (p // 2) % 4
    c = p % 2
    zk = z + 1 - 2 * (z % 2)
    zq = (z + 3 + 2 * (z % 2)) % 4

    def dev(xx, yy, zz, cc):
        return (xx * 32 + yy * 8 + zz * 2 + cc, h)

    partner = (p, 1 - h)
    other = dev(x, y, z, 1 - c)
    beside = ((1 - x) * 32 + y * 8 + z * 2 + c, 1 - h)

    def kv_dev(dz, dy, cc):
        return dev(x, (y + dy) % 4, zk if dz else z, cc)

    def q_dev(r, cc):
        return dev(1 - x if r % 2 else x, y, zq if r // 2 else z, cc)

    def remote(src, dst, ss, rs, to):
        return pltpu.make_async_remote_copy(
            src_ref=src, dst_ref=dst, send_sem=ss, recv_sem=rs, device_id=to, device_id_type=MESH
        )

    loads = [
        pltpu.make_async_copy(hidden_ref, hid.at[h], lsem.at[0]),
        pltpu.make_async_copy(table_ref, table, lsem.at[1]),
        pltpu.make_async_copy(wqkv_ref.at[0], w.at[0], lsem.at[2]),
        pltpu.make_async_copy(wqkv_ref.at[1], w.at[1], lsem.at[3]),
        pltpu.make_async_copy(wqkv_ref.at[2], w.at[2], lsem.at[4]),
        pltpu.make_async_copy(wproj_ref.at[:, lanes_at(h * HALF, HALF)], wp, lsem.at[5]),
        pltpu.make_async_copy(stale_ref, stg.at[:, pl.ds(0, TOK)], lsem.at[6]),
        pltpu.make_async_copy(text_ref, txs, lsem.at[7]),
    ]
    for i in (6, 7, 0, 1):
        loads[i].start()

    barrier = pltpu.get_barrier_semaphore()
    peers = [partner, other, beside, kv_dev(0, 2, c)]
    for dz, dy in ((1, 0), (0, 1), (0, 3)):
        peers += [kv_dev(dz, dy, 0), kv_dev(dz, dy, 1)]
    for r in range(1, 4):
        peers += [q_dev(r, 0), q_dev(r, 1)]
    for peer in peers:
        pl.semaphore_signal(barrier, inc=1, device_id=peer, device_id_type=MESH)

    loads[6].wait()
    loads[7].wait()
    words = txs[...].astype(jnp.float32)
    key_tail = jnp.concatenate([words[0:8], words[0:8]], axis=0).astype(jnp.bfloat16)
    value_tail = jnp.concatenate([words[8:16], jnp.zeros((8, FEAT), jnp.float32)], axis=0).astype(jnp.bfloat16)
    stg[0, TOK:BLK, :] = key_tail
    stg[1, TOK:BLK, :] = value_tail
    fk[0, TOK:BLK, :] = key_tail
    fk[1, TOK:BLK, :] = value_tail

    pl.semaphore_wait(barrier, len(peers))

    sends = []

    def go(copy):
        copy.start()
        sends.append(copy)
        return copy

    hid_copies = [
        go(remote(hidden_ref.at[pl.ds(r0, n)], hid.at[h, pl.ds(r0, n)], hsend.at[i], hrecv.at[i], partner))
        for i, (r0, n) in enumerate(CHUNKS)
    ]

    def kv_lanes(j):
        return pl.ds(j * HD, HD)

    def own_blocks(j):
        rows = rows_at(stale_row(0, 0, c))
        pltpu.make_async_copy(
            stg.at[:, :, lanes_at(c * WIDE + j * HD, HD)], kvb.at[:, rows, kv_lanes(j)], kvrecv.at[c, j]
        ).start()
        k = 1
        for dz, dy in ((1, 0), (0, 1), (0, 3)):
            back = (4 - dy) % 4
            for cc in range(2):
                go(
                    remote(
                        stg.at[:, :, pl.ds(cc * WIDE + j * HD, HD)],
                        kvb.at[:, rows_at(stale_row(dz, back, c)), kv_lanes(j)],
                        kvsend.at[k, j], kvrecv.at[dz * 8 + back * 2 + c, j], kv_dev(dz, dy, cc),
                    )
                )
                k += 1
        go(
            remote(
                stg.at[:, :, lanes_at((1 - c) * WIDE + j * HD, HD)], kvb.at[:, rows, kv_lanes(j)],
                kvsend.at[0, j], kvrecv.at[c, j], other,
            )
        )

    def kv_wait(dz, dy, s, j):
        ref = kvb.at[:, rows_at(stale_row(dz, dy, s)), kv_lanes(j)]
        remote(ref, ref, kvsend.at[0, 0], kvrecv.at[dz * 8 + dy * 2 + s, j], other).wait_recv()

    def forward_plane(j):
        k = 7
        for s in range(2):
            kv_wait(1, 0, s, j)
            src = kvb.at[:, rows_at(stale_row(1, 0, s)), kv_lanes(j)]
            for dy in (1, 3):
                back = (4 - dy) % 4
                go(
                    remote(
                        src, kvb.at[:, rows_at(stale_row(1, back, s)), kv_lanes(j)],
                        kvsend.at[k, j], kvrecv.at[8 + back * 2 + s, j], kv_dev(0, dy, c),
                    )
                )
                k += 1

    def forward_far(j):
        k = 11
        for s, frm, to in ((0, 3, 1), (1, 1, 3)):
            kv_wait(0, frm, s, j)
            src = kvb.at[:, rows_at(stale_row(0, frm, s)), kv_lanes(j)]
            go(
                remote(
                    src, kvb.at[:, rows_at(stale_row(0, 2, s)), kv_lanes(j)],
                    kvsend.at[k, j], kvrecv.at[4 + s, j], kv_dev(0, to, c),
                )
            )
            k += 1

    def forward_z(j):
        for s in range(2):
            kv_wait(0, 2, s, j)
            go(
                remote(
                    kvb.at[:, rows_at(stale_row(0, 2, s)), kv_lanes(j)],
                    kvb.at[:, rows_at(stale_row(1, 2, s)), kv_lanes(j)],
                    kvsend.at[13 + s, j], kvrecv.at[12 + s, j], kv_dev(1, 0, c),
                )
            )

    for j in range(3):
        own_blocks(j)
    for i in (2, 3, 4, 5):
        loads[i].start()

    block = order_ref[p]
    pos = lax.broadcasted_iota(jnp.int32, (TOK, HD), 0) + block * TOK
    row_pos = (pos >> 8).astype(jnp.float32)
    col_pos = (pos & 255).astype(jnp.float32)
    angles = row_pos * freq_ref[0:1, :] + col_pos * freq_ref[1:2, :]
    lane = lax.broadcasted_iota(jnp.int32, (TOK, HD), 1)
    even = (lane & 1) == 0
    cost[...] = jnp.cos(angles)
    sine = jnp.sin(angles)
    sint[...] = jnp.where(even, -sine, sine)

    live = lax.broadcasted_iota(jnp.int32, (BLK, HD), 0) < LIVE
    for i in range(16):
        mask[i * BLK : (i + 1) * BLK, :] = jnp.where(live, 1.0, 0.0).astype(jnp.bfloat16)

    loads[1].wait()
    step = step_ref[0]
    modv[0:1, :] = table[0, pl.ds(step, 1), :]
    modv[1:2, :] = 1.0 + table[1, pl.ds(step, 1), :]
    modv[2:3, :] = table[2, pl.ds(step, 1), :]

    loads[0].wait()

    def layer_norm(i):
        r0, n = CHUNKS[i]
        hid_copies[i].wait_recv()

        rows = pl.ds(r0, n)
        a = hid[0, rows, :].astype(jnp.float32)
        b = hid[1, rows, :].astype(jnp.float32)
        mean = (jnp.sum(a, axis=1, keepdims=True) + jnp.sum(b, axis=1, keepdims=True)) * (1.0 / 3072)
        a = a - mean
        b = b - mean
        var = (jnp.sum(a * a, axis=1, keepdims=True) + jnp.sum(b * b, axis=1, keepdims=True)) * (1.0 / 3072)
        inv = lax.rsqrt(var + 1e-6)
        modded[rows, 0:HALF] = (modv[1:2, 0:HALF] * (a * inv) + modv[0:1, 0:HALF]).astype(jnp.bfloat16)
        modded[rows, HALF:] = (modv[1:2, HALF:] * (b * inv) + modv[0:1, HALF:]).astype(jnp.bfloat16)

    for i in range(4):
        layer_norm(i)
    forward_far(0)
    forward_plane(0)

    mine = pl.ds(pl.multiple_of(c * WIDE + y * PIECE, 16), PIECE)
    go(
        remote(
            wproj_ref.at[mine, lanes_at((1 - h) * HALF, HALF)], wo.at[mine], wsend.at[0], wrecv.at[y], beside
        )
    )

    def piece_wait(d):
        yy = (y + d) % 4
        ref = wo.at[pl.ds(pl.multiple_of(c * WIDE + yy * PIECE, 16), PIECE)]
        remote(ref, ref, wsend.at[0], wrecv.at[yy], other).wait_recv()

    def head_out(v, which):
        mean_square = jnp.mean(v * v, axis=1, keepdims=True)
        v = v * lax.rsqrt(mean_square + 1e-6) * gain_ref[which : which + 1, :]
        swapped = jnp.where(even, pltpu.roll(v, 127, 1), pltpu.roll(v, 1, 1))
        return (v * cost[...] + swapped * sint[...]).astype(jnp.bfloat16)

    def send_queries(j):
        for r in (1, 2, 3):
            for cc in range(2):
                g = cc * 3 + j
                go(remote(qs.at[g], qb.at[j, 2 * r + c], qsend.at[r, g], qrecv.at[j, 2 * r + c], q_dev(r, cc)))
        pltpu.make_async_copy(qs.at[c * 3 + j], qb.at[j, c], qrecv.at[j, c]).start()
        go(remote(qs.at[(1 - c) * 3 + j], qb.at[j, c], qsend.at[0, j], qrecv.at[j, c], other))

    for part in range(3):
        loads[2 + part].wait()
        for g2 in range(3):
            cols = pl.ds(g2 * 256, 256)
            acc = jnp.dot(modded[...], w[part, :, cols], preferred_element_type=jnp.float32)
            if part == 2:
                fk[1, 0:TOK, cols] = acc.astype(jnp.bfloat16)
                continue
            for i in range(2):
                g = g2 * 2 + i
                res = head_out(acc[:, i * HD : (i + 1) * HD], part)
                if part == 1:
                    fk[0, 0:TOK, g * HD : (g + 1) * HD] = res
                    continue
                qs[g] = res
        if part == 0:
            send_queries(0)
            forward_far(1)
            forward_far(2)

    fresh_row = rows_at(c * (17 * BLK))
    pltpu.make_async_copy(fk.at[:, :, lanes_at(c * WIDE, WIDE)], kvb.at[:, fresh_row, :], fsem.at[c]).start()
    go(
        remote(
            fk.at[:, :, lanes_at((1 - c) * WIDE, WIDE)], kvb.at[:, fresh_row, :], fsend.at[0], fsem.at[c], other
        )
    )
    fresh_out = pltpu.make_async_copy(fk.at[:, pl.ds(0, TOK)], fresh_ref, lsem.at[8])
    fresh_out.start()
    send_queries(1)
    forward_plane(1)
    forward_z(0)
    forward_plane(2)

    eye = lax.broadcasted_iota(jnp.int32, (128, 128), 0) == lax.broadcasted_iota(jnp.int32, (128, 128), 1)

    def q_wait(j, sub):
        remote(qb.at[j, sub], qb.at[j, sub], qsend.at[0, 0], qrecv.at[j, sub], other).wait_recv()

    def kv_wait_all(j):
        for dz in range(2):
            for dy in range(4):
                for s in range(2):
                    if (dz == 1 and dy == 0) or (dz == 0 and (dy == 2 or (dy, s) in ((3, 0), (1, 1)))):
                        continue
                    kv_wait(dz, dy, s, j)

    def qk(j, r, s):
        if r == 0:
            for u in range(2):
                s[u * TOK : (u + 1) * TOK, :] = lax.dot_general(
                    qb[j, u], kvb[0, pl.ds(2 * BLK * u, KEYS), kv_lanes(j)], NT,
                    preferred_element_type=jnp.float32,
                )
        else:
            q = qb[j, 2 * r : 2 * r + 2].reshape(2 * TOK, HD)
            s[...] = lax.dot_general(
                q, kvb[0, pl.ds(BLK, KEYS), kv_lanes(j)], NT, preferred_element_type=jnp.float32
            )

    def pv(j, r, s):
        scores = s[...]
        top = jnp.max(scores, axis=1, keepdims=True) * SCORE
        e = jnp.exp2(scores * SCORE - top).astype(jnp.bfloat16)
        if r == 0:
            accs = []
            for u in range(2):
                vals = jnp.concatenate([kvb[1, pl.ds(2 * BLK * u, KEYS), kv_lanes(j)], mask[...]], axis=1)
                accs.append(jnp.dot(e[u * TOK : (u + 1) * TOK], vals, preferred_element_type=jnp.float32))
        else:
            vals = jnp.concatenate([kvb[1, pl.ds(BLK, KEYS), kv_lanes(j)], mask[...]], axis=1)
            acc = jnp.dot(e, vals, preferred_element_type=jnp.float32)
            accs = [acc[:TOK], acc[TOK:]]
        for u in range(2):
            acc = accs[u]
            total = acc[:, HD:]
            ob[j, 2 * r + u, 0:TOK, :] = (acc[:, :HD] / total).astype(jnp.bfloat16)
            level = top[u * TOK : (u + 1) * TOK] + jnp.log2(total)
            la = jnp.sum(jnp.where(eye, level[:128], 0.0), axis=0, keepdims=True)
            lb = jnp.sum(jnp.where(eye[:48], level[128:], 0.0), axis=0, keepdims=True)
            rest = jnp.concatenate([la, lb], axis=0)
            terms = []
            for _ in range(3):
                term = rest.astype(jnp.bfloat16).astype(jnp.float32)
                terms.append(term)
                rest = rest - term
            terms.append(jnp.zeros((10, HD), jnp.float32))
            ob[j, 2 * r + u, TOK:BLK, :] = jnp.concatenate(terms, axis=0).astype(jnp.bfloat16)

    def o_copy(j, r, u):
        g = 3 * c + j
        return remote(ob.at[j, 2 * r + u], orx.at[g, r], osend.at[j, 2 * r + u], orecv.at[g, r], q_dev(r, u))

    def o_send(j, r):
        if r == 0:
            g = 3 * c + j
            pltpu.make_async_copy(ob.at[j, c], orx.at[g, 0], orecv.at[g, 0]).start()
            go(remote(ob.at[j, 1 - c], orx.at[g, 0], osend.at[j, 0], orecv.at[g, 0], other))
        else:
            go(o_copy(j, r, 0))
            go(o_copy(j, r, 1))

    att_copies = []

    def merge(j):
        for cc in range(2):
            for r in range(4):
                g = 3 * cc + j
                remote(orx.at[g, r], orx.at[g, r], osend.at[0, 0], orecv.at[g, r], other).wait_recv()
        for cc in range(2):
            g = 3 * cc + j
            levels = []
            for r in range(4):
                tail = orx[g, r, TOK:BLK, :].astype(jnp.float32)
                levels.append(tail[0:2] + tail[2:4] + tail[4:6])
            most = jnp.maximum(jnp.maximum(levels[0], levels[1]), jnp.maximum(levels[2], levels[3]))
            weights = [jnp.exp2(v - most) for v in levels]
            total = weights[0] + weights[1] + weights[2] + weights[3]
            merged_a = jnp.zeros((128, HD), jnp.float32)
            merged_b = jnp.zeros((48, HD), jnp.float32)
            for r in range(4):
                share = weights[r] / total
                col_a = jnp.sum(jnp.where(eye, share[0:1], 0.0), axis=1, keepdims=True)
                col_b = jnp.sum(jnp.where(eye[:48], share[1:2], 0.0), axis=1, keepdims=True)
                part = orx[g, r, 0:TOK, :].astype(jnp.float32)
                merged_a = merged_a + part[:128] * col_a
                merged_b = merged_b + part[128:] * col_b
            att[h, j, 0:128, cc * HD : (cc + 1) * HD] = merged_a.astype(jnp.bfloat16)
            att[h, j, 128:TOK, cc * HD : (cc + 1) * HD] = merged_b.astype(jnp.bfloat16)
        att_copies.append(go(remote(att.at[h, j], att.at[h, j], asend.at[j], arecv.at[j], partner)))

    for s in range(2):
        ref = kvb.at[:, pl.ds(s * 17 * BLK, BLK), :]
        remote(ref, ref, fsend.at[0], fsem.at[s], other).wait_recv()
    units = [(0, r) for r in (0, 1, 2, 3)] + [(1, r) for r in (0, 1, 2, 3)] + [(2, r) for r in (1, 2, 3, 0)]

    def score(i):
        j, r = units[i]
        if i % 4 == 0:
            kv_wait_all(j)
        q_wait(j, 2 * r)
        q_wait(j, 2 * r + 1)
        qk(j, r, s2 if i % 2 else s1)

    score(0)
    for i in range(12):
        if i < 11:
            score(i + 1)
        pv(*units[i], s2 if i % 2 else s1)
        o_send(*units[i])
        if i == 0:
            send_queries(2)
            forward_z(1)
        elif i == 1:
            forward_z(2)
        elif i == 4:
            piece_wait(0)
            for d in (1, 3, 2):
                go(remote(wo.at[mine], wo.at[mine], wsend.at[d], wrecv.at[y], kv_dev(0, d, c)))
        elif i == 6:
            merge(0)
        elif i == 10:
            merge(1)
    def rows_of(weights, j, cols):
        return jnp.concatenate(
            [weights[j * HD : (j + 1) * HD, cols], weights[WIDE + j * HD : WIDE + (j + 1) * HD, cols]], axis=0
        )

    def project(pairs, first):
        for i in range(3):
            cols = pl.ds(i * 512, 512)
            acc = None if first else pown[:, cols]
            for grp, weights, j in pairs:
                term = jnp.dot(att[grp, j], rows_of(weights, j, cols), preferred_element_type=jnp.float32)
                acc = term if acc is None else acc + term
            pown[:, cols] = acc

    for d in (1, 3, 2):
        piece_wait(d)
    half = wo.at[rows_at(c * WIDE, WIDE)]
    go(remote(half, half, wsend.at[4], wrecv.at[4], other))

    loads[5].wait()
    project([(h, wp, 0), (h, wp, 1)], True)
    merge(2)
    half = wo.at[rows_at((1 - c) * WIDE, WIDE)]
    remote(half, half, wsend.at[4], wrecv.at[4], other).wait_recv()
    att_copies[0].wait_recv()
    att_copies[1].wait_recv()
    project([(h, wp, 2), (1 - h, wo, 0), (1 - h, wo, 1)], False)
    att_copies[2].wait_recv()
    out_copies = []
    for i in range(3):
        cols = pl.ds(i * 512, 512)
        gate = modv[2:3, lanes_at(h * HALF + i * 512, 512)]
        summed = pown[:, cols] + jnp.dot(att[1 - h, 2], rows_of(wo, 2, cols), preferred_element_type=jnp.float32)
        outb[:, cols] = (hid[h, :, cols].astype(jnp.float32) + gate * summed).astype(jnp.bfloat16)
        cp = pltpu.make_async_copy(outb.at[:, cols], out_ref.at[:, cols], lsem.at[9 + i])
        cp.start()
        out_copies.append(cp)

    for cp in sends:
        cp.wait_send()
    fresh_out.wait()
    for cp in out_copies:
        cp.wait()


def copy_kernel(a_ref, b_ref, c_ref, d_ref, a, b, sem):
    pairs = [
        (a_ref.at[pl.ds(r, n)], a.at[pl.ds(r, n)], c_ref.at[pl.ds(r, n)]) for r, n in ((0, 96), (96, 80))
    ]
    pairs += [(b_ref.at[i], b.at[i], d_ref.at[i]) for i in range(2)]
    ins = [pltpu.make_async_copy(src, mid, sem.at[i]) for i, (src, mid, _) in enumerate(pairs)]
    outs = [pltpu.make_async_copy(mid, dst, sem.at[4 + i]) for i, (_, mid, dst) in enumerate(pairs)]
    for cp in ins:
        cp.start()
    for cp_in, cp_out in zip(ins, outs):
        cp_in.wait()
        cp_out.start()
    for cp in outs:
        cp.wait()


def frequencies():
    freq = np.power(10000.0, -2.0 * np.arange(28) / 56.0).astype(np.float32)
    both = np.zeros((2, 64), np.float32)
    both[0, 8:36] = freq
    both[1, 36:64] = freq
    return np.repeat(both, 2, axis=1)


def body(
    image_hidden, mod_table, step_index, qkv_weight, norm_gain, proj_weight, stale_kv, text_kv, patch_order
):
    bf, f32 = jnp.bfloat16, jnp.float32
    anywhere = pl.BlockSpec(memory_space=pl.ANY)
    vmem = pl.BlockSpec(memory_space=pltpu.VMEM)
    smem = pl.BlockSpec(memory_space=pltpu.SMEM)
    V = pltpu.VMEM
    S = pltpu.SemaphoreType.DMA
    scratch = [
        V((3, 3072, FEAT), bf),
        V((FEAT, HALF), bf),
        V((FEAT, HALF), bf),
        V((3, 28, 3072), f32),
        V((8, 3072), f32),
        V((2, TOK, HALF), bf),
        V((TOK, 3072), bf),
        V((6, TOK, HD), bf),
        V((3, 8, TOK, HD), bf),
        V((2, KROWS, WIDE), bf),
        V((2, BLK, FEAT), bf),
        V((16, FEAT), bf),
        V((2, BLK, FEAT), bf),
        V((KEYS, HD), bf),
        V((TOK, HD), f32),
        V((TOK, HD), f32),
        V((2 * TOK, KEYS), f32),
        V((2 * TOK, KEYS), f32),
        V((3, 8, BLK, HD), bf),
        V((6, 4, BLK, HD), bf),
        V((2, 3, TOK, 2 * HD), bf),
        V((TOK, HALF), f32),
        V((TOK, HALF), bf),
        S((12,)),
        S((4,)), S((4,)),
        S((15, 3)), S((16, 3)),
        S((2,)), S((1,)),
        S((4, 6)), S((3, 8)),
        S((3, 8)), S((6, 4)),
        S((5,)), S((5,)),
        S((3,)), S((3,)),
    ]
    call = pl.pallas_call(
        kernel,
        out_shape=(
            jax.ShapeDtypeStruct((TOK, HALF), bf),
            jax.ShapeDtypeStruct((2, TOK, FEAT), bf),
        ),
        in_specs=[
            anywhere, anywhere, smem, anywhere, vmem, anywhere, anywhere, anywhere, smem, vmem,
        ],
        out_specs=(anywhere, anywhere),
        scratch_shapes=scratch,
        compiler_params=pltpu.CompilerParams(
            collective_id=0, has_side_effects=True, vmem_limit_bytes=58 * 2**20
        ),
        cost_estimate=pl.CostEstimate(flops=10**10, bytes_accessed=2 * 10**7, transcendentals=13 * 10**6),
    )
    image_out, fresh_kv = call(
        image_hidden,
        jnp.transpose(mod_table, (1, 0, 2)),
        step_index,
        jnp.transpose(qkv_weight, (1, 0, 2)),
        norm_gain,
        proj_weight,
        stale_kv,
        text_kv.reshape(16, FEAT),
        patch_order,
        jnp.asarray(frequencies()),
    )
    return pl.pallas_call(
        copy_kernel,
        out_shape=(
            jax.ShapeDtypeStruct((TOK, HALF), bf),
            jax.ShapeDtypeStruct((2, TOK, FEAT), bf),
        ),
        in_specs=[anywhere, anywhere],
        out_specs=(anywhere, anywhere),
        scratch_shapes=[V((TOK, HALF), bf), V((2, TOK, FEAT), bf), S((8,))],
        compiler_params=pltpu.CompilerParams(vmem_limit_bytes=58 * 2**20),
    )(image_out, fresh_kv)


def solution(mesh):
    return jax.shard_map(
        body,
        mesh=mesh,
        in_specs=(
            P("patch", "head"),
            P(),
            P(),
            P(None, None, "head"),
            P(),
            P("head", None),
            P(None, "patch", "head"),
            P(None, "patch", "head"),
            P(),
        ),
        out_specs=(P("patch", "head"), P(None, "patch", "head")),
        check_vma=False,
    )
```

```python
import functools

import jax
import jax.numpy as jnp
import numpy as np
from jax import lax
from jax.experimental import pallas as pl
from jax.experimental.pallas import tpu as pltpu
from jax.sharding import PartitionSpec as P

MESH = pl.DeviceIdType.MESH
TOK = 176
BLK = 192
LIVE = 184
HALF = 1536
FEAT = 768
WIDE = 384
HD = 128
KEYS = 16 * BLK
KROWS = 18 * BLK
PIECE = 192
LOG2E = 1.4426950408889634
SCORE = LOG2E / 128.0**0.5
CHUNKS = ((0, 48), (48, 48), (96, 48), (144, 32))
NT = (((1,), (1,)), ((), ()))


def stale_row(dz, dy, s):
    if dz == 0 and dy == 0:
        return jnp.where(s == 0, 16 * BLK, BLK) if not isinstance(s, int) else (16 * BLK, BLK)[s]
    if dz == 0:
        return (2 + (dy - 1) * 2 + s) * BLK
    return (8 + dy * 2 + s) * BLK


def rows_at(start, n=BLK):
    if isinstance(start, int):
        return pl.ds(start, n)
    return pl.ds(pl.multiple_of(start, 16), n)


def lanes_at(start, n):
    if isinstance(start, int):
        return pl.ds(start, n)
    return pl.ds(pl.multiple_of(start, 128), n)


def kernel(
    hidden_ref, table_ref, step_ref, wqkv_ref, gain_ref, wproj_ref, stale_ref, text_ref, order_ref, freq_ref,
    out_ref, fresh_ref,
    w, wp, wo, table, modv, hid, modded, qs, qb, kvb, stg, txs, fk, mask, cost, sint,
    s1, s2, ob, orx, att, pown, outb,
    lsem, hsend, hrecv, kvsend, kvrecv, fsem, fsend, qsend, qrecv,
    osend, orecv, wsend, wrecv, asend, arecv,
):
    p = lax.axis_index("patch")
    h = lax.axis_index("head")
    x = p // 32
    y = (p // 8) % 4
    z = (p // 2) % 4
    c = p % 2
    zk = z + 1 - 2 * (z % 2)
    zq = (z + 3 + 2 * (z % 2)) % 4

    def dev(xx, yy, zz, cc):
        return (xx * 32 + yy * 8 + zz * 2 + cc, h)

    partner = (p, 1 - h)
    other = dev(x, y, z, 1 - c)
    beside = ((1 - x) * 32 + y * 8 + z * 2 + c, 1 - h)

    def kv_dev(dz, dy, cc):
        return dev(x, (y + dy) % 4, zk if dz else z, cc)

    def q_dev(r, cc):
        return dev(1 - x if r % 2 else x, y, zq if r // 2 else z, cc)

    def remote(src, dst, ss, rs, to):
        return pltpu.make_async_remote_copy(
            src_ref=src, dst_ref=dst, send_sem=ss, recv_sem=rs, device_id=to, device_id_type=MESH
        )

    loads = [
        pltpu.make_async_copy(hidden_ref, hid.at[h], lsem.at[0]),
        pltpu.make_async_copy(table_ref, table, lsem.at[1]),
        pltpu.make_async_copy(wqkv_ref.at[0], w.at[0], lsem.at[2]),
        pltpu.make_async_copy(wqkv_ref.at[1], w.at[1], lsem.at[3]),
        pltpu.make_async_copy(wqkv_ref.at[2], w.at[2], lsem.at[4]),
        pltpu.make_async_copy(wproj_ref.at[:, lanes_at(h * HALF, HALF)], wp, lsem.at[5]),
        pltpu.make_async_copy(stale_ref, stg.at[:, pl.ds(0, TOK)], lsem.at[6]),
        pltpu.make_async_copy(text_ref, txs, lsem.at[7]),
    ]
    for i in (6, 7, 0, 1):
        loads[i].start()

    barrier = pltpu.get_barrier_semaphore()
    peers = [partner, other, beside]
    for dz, dy in ((1, 0), (0, 1), (0, 3)):
        peers += [kv_dev(dz, dy, 0), kv_dev(dz, dy, 1)]
    for r in range(1, 4):
        peers += [q_dev(r, 0), q_dev(r, 1)]
    for peer in peers:
        pl.semaphore_signal(barrier, inc=1, device_id=peer, device_id_type=MESH)

    pl.semaphore_wait(barrier, len(peers))

    sends = []

    def go(copy):
        copy.start()
        sends.append(copy)
        return copy

    hid_copies = [
        go(remote(hidden_ref.at[pl.ds(r0, n)], hid.at[h, pl.ds(r0, n)], hsend.at[i], hrecv.at[i], partner))
        for i, (r0, n) in enumerate(CHUNKS)
    ]

    loads[6].wait()
    loads[7].wait()
    words = txs[...].astype(jnp.float32)
    key_tail = jnp.concatenate([words[0:8], words[0:8]], axis=0).astype(jnp.bfloat16)
    value_tail = jnp.concatenate([words[8:16], jnp.zeros((8, FEAT), jnp.float32)], axis=0).astype(jnp.bfloat16)
    stg[0, TOK:BLK, :] = key_tail
    stg[1, TOK:BLK, :] = value_tail
    fk[0, TOK:BLK, :] = key_tail
    fk[1, TOK:BLK, :] = value_tail

    def kv_lanes(j):
        return pl.ds(j * HD, HD)

    def own_blocks(j):
        rows = rows_at(stale_row(0, 0, c))
        pltpu.make_async_copy(
            stg.at[:, :, lanes_at(c * WIDE + j * HD, HD)], kvb.at[:, rows, kv_lanes(j)], kvrecv.at[c, j]
        ).start()
        k = 1
        for dz, dy in ((1, 0), (0, 1), (0, 3)):
            back = (4 - dy) % 4
            for cc in range(2):
                go(
                    remote(
                        stg.at[:, :, pl.ds(cc * WIDE + j * HD, HD)],
                        kvb.at[:, rows_at(stale_row(dz, back, c)), kv_lanes(j)],
                        kvsend.at[k, j], kvrecv.at[dz * 8 + back * 2 + c, j], kv_dev(dz, dy, cc),
                    )
                )
                k += 1
        go(
            remote(
                stg.at[:, :, lanes_at((1 - c) * WIDE + j * HD, HD)], kvb.at[:, rows, kv_lanes(j)],
                kvsend.at[0, j], kvrecv.at[c, j], other,
            )
        )

    def kv_wait(dz, dy, s, j):
        ref = kvb.at[:, rows_at(stale_row(dz, dy, s)), kv_lanes(j)]
        remote(ref, ref, kvsend.at[0, 0], kvrecv.at[dz * 8 + dy * 2 + s, j], other).wait_recv()

    def forward_plane(j):
        k = 7
        for s in range(2):
            kv_wait(1, 0, s, j)
            src = kvb.at[:, rows_at(stale_row(1, 0, s)), kv_lanes(j)]
            for dy in (1, 3):
                back = (4 - dy) % 4
                go(
                    remote(
                        src, kvb.at[:, rows_at(stale_row(1, back, s)), kv_lanes(j)],
                        kvsend.at[k, j], kvrecv.at[8 + back * 2 + s, j], kv_dev(0, dy, c),
                    )
                )
                k += 1

    def forward_far(j):
        k = 11
        for s, frm, to in ((0, 3, 1), (1, 1, 3)):
            kv_wait(0, frm, s, j)
            src = kvb.at[:, rows_at(stale_row(0, frm, s)), kv_lanes(j)]
            go(
                remote(
                    src, kvb.at[:, rows_at(stale_row(0, 2, s)), kv_lanes(j)],
                    kvsend.at[k, j], kvrecv.at[4 + s, j], kv_dev(0, to, c),
                )
            )
            k += 1

    def forward_z(j):
        for s in range(2):
            kv_wait(0, 2, s, j)
            go(
                remote(
                    kvb.at[:, rows_at(stale_row(0, 2, s)), kv_lanes(j)],
                    kvb.at[:, rows_at(stale_row(1, 2, s)), kv_lanes(j)],
                    kvsend.at[13 + s, j], kvrecv.at[12 + s, j], kv_dev(1, 0, c),
                )
            )

    own_blocks(0)
    for i in (2, 3, 4, 5):
        loads[i].start()

    block = order_ref[p]
    pos = lax.broadcasted_iota(jnp.int32, (TOK, HD), 0) + block * TOK
    row_pos = (pos >> 8).astype(jnp.float32)
    col_pos = (pos & 255).astype(jnp.float32)
    angles = row_pos * freq_ref[0:1, :] + col_pos * freq_ref[1:2, :]
    lane = lax.broadcasted_iota(jnp.int32, (TOK, HD), 1)
    even = (lane & 1) == 0
    cost[...] = jnp.cos(angles)
    sine = jnp.sin(angles)
    sint[...] = jnp.where(even, -sine, sine)

    own_blocks(1)

    live = lax.broadcasted_iota(jnp.int32, (BLK, HD), 0) < LIVE
    for i in range(16):
        mask[i * BLK : (i + 1) * BLK, :] = jnp.where(live, 1.0, 0.0).astype(jnp.bfloat16)

    loads[1].wait()
    step = step_ref[0]
    modv[0:1, :] = table[0, pl.ds(step, 1), :]
    modv[1:2, :] = 1.0 + table[1, pl.ds(step, 1), :]
    modv[2:3, :] = table[2, pl.ds(step, 1), :]

    loads[0].wait()

    def layer_norm(i):
        r0, n = CHUNKS[i]
        hid_copies[i].wait_recv()

        rows = pl.ds(r0, n)
        a = hid[0, rows, :].astype(jnp.float32)
        b = hid[1, rows, :].astype(jnp.float32)
        mean = (jnp.sum(a, axis=1, keepdims=True) + jnp.sum(b, axis=1, keepdims=True)) * (1.0 / 3072)
        a = a - mean
        b = b - mean
        var = (jnp.sum(a * a, axis=1, keepdims=True) + jnp.sum(b * b, axis=1, keepdims=True)) * (1.0 / 3072)
        inv = lax.rsqrt(var + 1e-6)
        modded[rows, 0:HALF] = (modv[1:2, 0:HALF] * (a * inv) + modv[0:1, 0:HALF]).astype(jnp.bfloat16)
        modded[rows, HALF:] = (modv[1:2, HALF:] * (b * inv) + modv[0:1, HALF:]).astype(jnp.bfloat16)

    forward_far(0)
    forward_plane(0)
    own_blocks(2)
    for i in range(4):
        layer_norm(i)

    def wo_rows(parity, first=0, n=PIECE):
        return wo.at[pl.ds(pl.multiple_of(c * WIDE + parity * PIECE + first, 16), n)]

    odd = y % 2
    mine = pl.ds(pl.multiple_of(c * WIDE + odd * PIECE, 16), PIECE)
    go(remote(wproj_ref.at[mine, lanes_at((1 - h) * HALF, HALF)], wo_rows(odd), wsend.at[0], wrecv.at[0], beside))

    def weight_gather():
        remote(wo_rows(odd), wo_rows(odd), wsend.at[0], wrecv.at[0], other).wait_recv()
        for i, dy in enumerate((1, 3)):
            part = wo_rows(odd, i * 96, 96)
            go(remote(part, part, wsend.at[1 + i], wrecv.at[1 + i], kv_dev(0, dy, c)))
        go(remote(wo_rows(odd), wo_rows(odd), wsend.at[3], wrecv.at[3], other))

    def weight_share():
        for i in range(2):
            part = wo_rows(1 - odd, i * 96, 96)
            remote(part, part, wsend.at[0], wrecv.at[1 + i], other).wait_recv()
        go(remote(wo_rows(1 - odd), wo_rows(1 - odd), wsend.at[4], wrecv.at[4], other))

    def weight_wait():
        for i in (3, 4):
            remote(wo_rows(odd), wo_rows(odd), wsend.at[0], wrecv.at[i], other).wait_recv()

    def head_out(v, which):
        mean_square = jnp.mean(v * v, axis=1, keepdims=True)
        v = v * lax.rsqrt(mean_square + 1e-6) * gain_ref[which : which + 1, :]
        swapped = jnp.where(even, pltpu.roll(v, 127, 1), pltpu.roll(v, 1, 1))
        return (v * cost[...] + swapped * sint[...]).astype(jnp.bfloat16)

    def send_queries(j):
        for r in (1, 2, 3):
            for cc in range(2):
                g = cc * 3 + j
                go(remote(qs.at[g], qb.at[j, 2 * r + c], qsend.at[r, g], qrecv.at[j, 2 * r + c], q_dev(r, cc)))
        pltpu.make_async_copy(qs.at[c * 3 + j], qb.at[j, c], qrecv.at[j, c]).start()
        go(remote(qs.at[(1 - c) * 3 + j], qb.at[j, c], qsend.at[0, j], qrecv.at[j, c], other))

    loads[2].wait()
    for j in range(3):
        pair = jnp.concatenate([w[0, :, j * HD : (j + 1) * HD], w[0, :, WIDE + j * HD : WIDE + (j + 1) * HD]], axis=1)
        acc = jnp.dot(modded[...], pair, preferred_element_type=jnp.float32)
        qs[j] = head_out(acc[:, :HD], 0)
        qs[3 + j] = head_out(acc[:, HD:], 0)
        if j == 0:
            send_queries(0)
    forward_z(0)
    forward_far(1)
    forward_plane(1)
    for part in (1, 2):
        loads[2 + part].wait()
        for g2 in range(3):
            cols = pl.ds(g2 * 256, 256)
            acc = jnp.dot(modded[...], w[part, :, cols], preferred_element_type=jnp.float32)
            if part == 2:
                fk[1, 0:TOK, cols] = acc.astype(jnp.bfloat16)
                continue
            for i in range(2):
                g = g2 * 2 + i
                fk[0, 0:TOK, g * HD : (g + 1) * HD] = head_out(acc[:, i * HD : (i + 1) * HD], 1)

    fresh_row = rows_at(c * (17 * BLK))
    pltpu.make_async_copy(fk.at[:, :, lanes_at(c * WIDE, WIDE)], kvb.at[:, fresh_row, :], fsem.at[c]).start()
    go(
        remote(
            fk.at[:, :, lanes_at((1 - c) * WIDE, WIDE)], kvb.at[:, fresh_row, :], fsend.at[0], fsem.at[c], other
        )
    )
    fresh_out = pltpu.make_async_copy(fk.at[:, pl.ds(0, TOK)], fresh_ref, lsem.at[8])
    fresh_out.start()
    forward_far(2)
    forward_plane(2)
    send_queries(1)

    eye = lax.broadcasted_iota(jnp.int32, (128, 128), 0) == lax.broadcasted_iota(jnp.int32, (128, 128), 1)

    def q_wait(j, sub):
        remote(qb.at[j, sub], qb.at[j, sub], qsend.at[0, 0], qrecv.at[j, sub], other).wait_recv()

    def kv_wait_all(j):
        for dz in range(2):
            for dy in range(4):
                for s in range(2):
                    if (dz == 1 and dy == 0) or (dz == 0 and (dy == 2 or (dy, s) in ((3, 0), (1, 1)))):
                        continue
                    kv_wait(dz, dy, s, j)

    def qk(j, r, s):
        if r == 0:
            for u in range(2):
                s[u * TOK : (u + 1) * TOK, :] = lax.dot_general(
                    qb[j, u], kvb[0, pl.ds(2 * BLK * u, KEYS), kv_lanes(j)], NT,
                    preferred_element_type=jnp.float32,
                )
        else:
            q = qb[j, 2 * r : 2 * r + 2].reshape(2 * TOK, HD)
            s[...] = lax.dot_general(
                q, kvb[0, pl.ds(BLK, KEYS), kv_lanes(j)], NT, preferred_element_type=jnp.float32
            )

    def pv(j, r, s):
        scores = s[...]
        top = jnp.max(scores, axis=1, keepdims=True) * SCORE
        e = jnp.exp2(scores * SCORE - top).astype(jnp.bfloat16)
        if r == 0:
            accs = []
            for u in range(2):
                vals = jnp.concatenate([kvb[1, pl.ds(2 * BLK * u, KEYS), kv_lanes(j)], mask[...]], axis=1)
                accs.append(jnp.dot(e[u * TOK : (u + 1) * TOK], vals, preferred_element_type=jnp.float32))
        else:
            vals = jnp.concatenate([kvb[1, pl.ds(BLK, KEYS), kv_lanes(j)], mask[...]], axis=1)
            acc = jnp.dot(e, vals, preferred_element_type=jnp.float32)
            accs = [acc[:TOK], acc[TOK:]]
        for u in range(2):
            acc = accs[u]
            total = acc[:, HD:]
            ob[j, 2 * r + u, 0:TOK, :] = (acc[:, :HD] / total).astype(jnp.bfloat16)
            level = top[u * TOK : (u + 1) * TOK] + jnp.log2(total)
            la = jnp.sum(jnp.where(eye, level[:128], 0.0), axis=0, keepdims=True)
            lb = jnp.sum(jnp.where(eye[:48], level[128:], 0.0), axis=0, keepdims=True)
            rest = jnp.concatenate([la, lb], axis=0)
            terms = []
            for _ in range(3):
                term = rest.astype(jnp.bfloat16).astype(jnp.float32)
                terms.append(term)
                rest = rest - term
            terms.append(jnp.zeros((10, HD), jnp.float32))
            ob[j, 2 * r + u, TOK:BLK, :] = jnp.concatenate(terms, axis=0).astype(jnp.bfloat16)

    def o_copy(j, r, u):
        g = 3 * c + j
        return remote(ob.at[j, 2 * r + u], orx.at[g, r], osend.at[j, 2 * r + u], orecv.at[g, r], q_dev(r, u))

    def o_send(j, r):
        if r == 0:
            g = 3 * c + j
            pltpu.make_async_copy(ob.at[j, c], orx.at[g, 0], orecv.at[g, 0]).start()
            go(remote(ob.at[j, 1 - c], orx.at[g, 0], osend.at[j, 0], orecv.at[g, 0], other))
        else:
            go(o_copy(j, r, 0))
            go(o_copy(j, r, 1))

    att_copies = []

    def merge(j):
        for cc in range(2):
            for r in range(4):
                g = 3 * cc + j
                remote(orx.at[g, r], orx.at[g, r], osend.at[0, 0], orecv.at[g, r], other).wait_recv()
        for cc in range(2):
            g = 3 * cc + j
            levels = []
            for r in range(4):
                tail = orx[g, r, TOK:BLK, :].astype(jnp.float32)
                levels.append(tail[0:2] + tail[2:4] + tail[4:6])
            most = jnp.maximum(jnp.maximum(levels[0], levels[1]), jnp.maximum(levels[2], levels[3]))
            weights = [jnp.exp2(v - most) for v in levels]
            total = weights[0] + weights[1] + weights[2] + weights[3]
            merged_a = jnp.zeros((128, HD), jnp.float32)
            merged_b = jnp.zeros((48, HD), jnp.float32)
            for r in range(4):
                share = weights[r] / total
                col_a = jnp.sum(jnp.where(eye, share[0:1], 0.0), axis=1, keepdims=True)
                col_b = jnp.sum(jnp.where(eye[:48], share[1:2], 0.0), axis=1, keepdims=True)
                part = orx[g, r, 0:TOK, :].astype(jnp.float32)
                merged_a = merged_a + part[:128] * col_a
                merged_b = merged_b + part[128:] * col_b
            att[h, j, 0:128, cc * HD : (cc + 1) * HD] = merged_a.astype(jnp.bfloat16)
            att[h, j, 128:TOK, cc * HD : (cc + 1) * HD] = merged_b.astype(jnp.bfloat16)
        att_copies.append(go(remote(att.at[h, j], att.at[h, j], asend.at[j], arecv.at[j], partner)))

    for s in range(2):
        ref = kvb.at[:, pl.ds(s * 17 * BLK, BLK), :]
        remote(ref, ref, fsend.at[0], fsem.at[s], other).wait_recv()
    units = [(0, r) for r in (0, 1, 2, 3)] + [(1, r) for r in (0, 1, 2, 3)] + [(2, r) for r in (1, 2, 3, 0)]

    def score(i):
        j, r = units[i]
        if i % 4 == 0:
            kv_wait_all(j)
        q_wait(j, 2 * r)
        q_wait(j, 2 * r + 1)
        qk(j, r, s2 if i % 2 else s1)

    score(0)
    early = 0
    for i in range(12):
        if i == 9:
            early = len(sends)
        if i < 11:
            score(i + 1)
        pv(*units[i], s2 if i % 2 else s1)
        o_send(*units[i])
        if i == 0:
            send_queries(2)
            forward_z(1)
        elif i == 3:
            forward_z(2)
        elif i == 4:
            weight_gather()
        elif i == 7:
            merge(0)
        elif i == 10:
            weight_share()
    def rows_of(weights, j, cols):
        return jnp.concatenate(
            [weights[j * HD : (j + 1) * HD, cols], weights[WIDE + j * HD : WIDE + (j + 1) * HD, cols]], axis=0
        )

    def project(pairs, first):
        for i in range(3):
            cols = pl.ds(i * 512, 512)
            acc = None if first else pown[:, cols]
            for grp, weights, j in pairs:
                term = jnp.dot(att[grp, j], rows_of(weights, j, cols), preferred_element_type=jnp.float32)
                acc = term if acc is None else acc + term
            pown[:, cols] = acc

    loads[5].wait()
    merge(1)
    project([(h, wp, 0), (h, wp, 1)], True)
    for cp in sends[:early]:
        cp.wait_send()
    merge(2)
    weight_wait()
    att_copies[0].wait_recv()
    att_copies[1].wait_recv()
    project([(h, wp, 2), (1 - h, wo, 0), (1 - h, wo, 1)], False)
    att_copies[2].wait_recv()
    out_copies = []
    for i in range(3):
        cols = pl.ds(i * 512, 512)
        gate = modv[2:3, lanes_at(h * HALF + i * 512, 512)]
        summed = pown[:, cols] + jnp.dot(att[1 - h, 2], rows_of(wo, 2, cols), preferred_element_type=jnp.float32)
        outb[:, cols] = (hid[h, :, cols].astype(jnp.float32) + gate * summed).astype(jnp.bfloat16)
        cp = pltpu.make_async_copy(outb.at[:, cols], out_ref.at[:, cols], lsem.at[9 + i])
        cp.start()
        out_copies.append(cp)

    for cp in sends[early:]:
        cp.wait_send()
    fresh_out.wait()
    for cp in out_copies:
        cp.wait()


def copy_kernel(a_ref, b_ref, c_ref, d_ref, a, b, sem):
    pairs = [
        (a_ref.at[pl.ds(r, n)], a.at[pl.ds(r, n)], c_ref.at[pl.ds(r, n)]) for r, n in ((0, 96), (96, 80))
    ]
    pairs += [(b_ref.at[i], b.at[i], d_ref.at[i]) for i in range(2)]
    ins = [pltpu.make_async_copy(src, mid, sem.at[i]) for i, (src, mid, _) in enumerate(pairs)]
    outs = [pltpu.make_async_copy(mid, dst, sem.at[4 + i]) for i, (_, mid, dst) in enumerate(pairs)]
    for cp in ins:
        cp.start()
    for cp_in, cp_out in zip(ins, outs):
        cp_in.wait()
        cp_out.start()
    for cp in outs:
        cp.wait()


def frequencies():
    freq = np.power(10000.0, -2.0 * np.arange(28) / 56.0).astype(np.float32)
    both = np.zeros((2, 64), np.float32)
    both[0, 8:36] = freq
    both[1, 36:64] = freq
    return np.repeat(both, 2, axis=1)


def body(
    image_hidden, mod_table, step_index, qkv_weight, norm_gain, proj_weight, stale_kv, text_kv, patch_order
):
    bf, f32 = jnp.bfloat16, jnp.float32
    anywhere = pl.BlockSpec(memory_space=pl.ANY)
    vmem = pl.BlockSpec(memory_space=pltpu.VMEM)
    smem = pl.BlockSpec(memory_space=pltpu.SMEM)
    V = pltpu.VMEM
    S = pltpu.SemaphoreType.DMA
    scratch = [
        V((3, 3072, FEAT), bf),
        V((FEAT, HALF), bf),
        V((FEAT, HALF), bf),
        V((3, 28, 3072), f32),
        V((8, 3072), f32),
        V((2, TOK, HALF), bf),
        V((TOK, 3072), bf),
        V((6, TOK, HD), bf),
        V((3, 8, TOK, HD), bf),
        V((2, KROWS, WIDE), bf),
        V((2, BLK, FEAT), bf),
        V((16, FEAT), bf),
        V((2, BLK, FEAT), bf),
        V((KEYS, HD), bf),
        V((TOK, HD), f32),
        V((TOK, HD), f32),
        V((2 * TOK, KEYS), f32),
        V((2 * TOK, KEYS), f32),
        V((3, 8, BLK, HD), bf),
        V((6, 4, BLK, HD), bf),
        V((2, 3, TOK, 2 * HD), bf),
        V((TOK, HALF), f32),
        V((TOK, HALF), bf),
        S((12,)),
        S((4,)), S((4,)),
        S((15, 3)), S((16, 3)),
        S((2,)), S((1,)),
        S((4, 6)), S((3, 8)),
        S((3, 8)), S((6, 4)),
        S((5,)), S((5,)),
        S((3,)), S((3,)),
    ]
    call = pl.pallas_call(
        kernel,
        out_shape=(
            jax.ShapeDtypeStruct((TOK, HALF), bf),
            jax.ShapeDtypeStruct((2, TOK, FEAT), bf),
        ),
        in_specs=[
            anywhere, anywhere, smem, anywhere, vmem, anywhere, anywhere, anywhere, smem, vmem,
        ],
        out_specs=(anywhere, anywhere),
        scratch_shapes=scratch,
        compiler_params=pltpu.CompilerParams(
            collective_id=0, has_side_effects=True, vmem_limit_bytes=58 * 2**20
        ),
        cost_estimate=pl.CostEstimate(flops=10**10, bytes_accessed=2 * 10**7, transcendentals=13 * 10**6),
    )
    image_out, fresh_kv = call(
        image_hidden,
        jnp.transpose(mod_table, (1, 0, 2)),
        step_index,
        jnp.transpose(qkv_weight, (1, 0, 2)),
        norm_gain,
        proj_weight,
        stale_kv,
        text_kv.reshape(16, FEAT),
        patch_order,
        jnp.asarray(frequencies()),
    )
    return pl.pallas_call(
        copy_kernel,
        out_shape=(
            jax.ShapeDtypeStruct((TOK, HALF), bf),
            jax.ShapeDtypeStruct((2, TOK, FEAT), bf),
        ),
        in_specs=[anywhere, anywhere],
        out_specs=(anywhere, anywhere),
        scratch_shapes=[V((TOK, HALF), bf), V((2, TOK, FEAT), bf), S((8,))],
        compiler_params=pltpu.CompilerParams(vmem_limit_bytes=58 * 2**20),
    )(image_out, fresh_kv)


def solution(mesh):
    return jax.shard_map(
        body,
        mesh=mesh,
        in_specs=(
            P("patch", "head"),
            P(),
            P(),
            P(None, None, "head"),
            P(),
            P("head", None),
            P(None, "patch", "head"),
            P(None, "patch", "head"),
            P(),
        ),
        out_specs=(P("patch", "head"), P(None, "patch", "head")),
        check_vma=False,
    )
```
